32 devices in a mesh: lead: 2 (over x), gy: 4 (over y, core), gx: 4 (over z).
Axes of the slice: x: 2, y: 2, z: 4, core: 2. Of those that a mesh axis runs over, the one named last changes fastest.
Arguments:
- inputs: bfloat16 [2, 256, 32, 256], P('lead', 'gy', 'gx'), may hold values from -6 to 6
- lead_ids: int32 [2], P('lead'), may hold values from 0 to 359
- film: float32 [360, 4, 256], replicated, may hold values from -3 to 3
- flat_weights: bfloat16 [2, 589824], P(None, ('lead', 'gy', 'gx')), may hold values from -0.25 to 0.25
- cotangent: bfloat16 [2, 256, 32, 256], P('lead', 'gy', 'gx'), may hold values from -6 to 6
Outputs:
- outputs: bfloat16 [2, 256, 32, 256], P('lead', 'gy', 'gx')
- weight_grad: float32 [589824], P(('lead', 'gy', 'gx'))
The draws below stay inside these ranges and needn't reach their ends.
All inputs are finite; a program needn't handle non-finite values.
Results may differ from the reference program's by a relative error of at most 0.0047.
Values may be sent and summed in bfloat16 or wider, within the bound.
No kernel may reach another device: no remote copies, remote signals or barrier semaphores. Data moves between devices by JAX's collectives and lax.ppermute only.
A program may use at most 64 MiB of HBM per device.

```python
import math
import jax
import jax.numpy as jnp
from jax import lax

CHANNEL_COUNT = 256
LEAD_TIMES = 360
TILE_R = 64
TILE_C = 8
FIRST_DILATION = 64
SECOND_DILATION = 128
LEADS = 2
GRID_ROWS = 256
GRID_COLUMNS = 32
FLAT = 589824
N_GY = 4
N_GX = 4


def block_levels(rng, shape, cuts, smallest, top_value):
    level, own = 1.0, jax.random.fold_in(rng, 6)
    for position, blocks in cuts:
        draws = jnp.exp(jax.random.uniform(jax.random.fold_in(own, position), (blocks,), jnp.float32, smallest / len(cuts), top_value / len(cuts)))
        level = level * jnp.repeat(draws, shape[position] // blocks).reshape([-1 if axis == position else 1 for axis in range(len(shape))])
    return level


def centred(own_key, shape, deviation, limit, cuts=(), dtype=jnp.bfloat16):
    factor_of = block_levels(own_key, shape, cuts, -0.22, 0.18) if cuts else 1.0
    values = jax.random.normal(own_key, shape, jnp.float32) * deviation * factor_of
    return jnp.minimum(jnp.maximum(values, -limit), limit).astype(dtype)


def setup_inputs(seed: int = 0) -> dict:
    key_of = jax.random.split(jax.random.key(seed), 6)
    inputs = centred(key_of[0], (LEADS, GRID_ROWS, GRID_COLUMNS, CHANNEL_COUNT), 1.0, 6.0, ((0, 2), (1, 4), (2, 4)))
    lead_ids = jax.random.randint(key_of[1], (LEADS,), 0, LEAD_TIMES).astype(jnp.int32)
    film = centred(key_of[2], (LEAD_TIMES, 4, CHANNEL_COUNT), 0.5, 3.0, (), jnp.float32)
    flat_weights = centred(key_of[3], (2, FLAT), (9 * CHANNEL_COUNT // 4) ** -0.5, 0.25, ((1, 32),))
    cotangent = centred(key_of[4], (LEADS, GRID_ROWS, GRID_COLUMNS, CHANNEL_COUNT), 1.0, 6.0, ((0, 2), (1, 4), (2, 4)))
    return {"inputs": inputs, "lead_ids": lead_ids, "film": film, "flat_weights": flat_weights, "cotangent": cotangent}


def shifted(weather_field, row_off, col_off, dilation):
    padded = jnp.pad(weather_field, ((dilation, dilation), (dilation, dilation), (0, 0)))
    top = dilation + row_off * dilation
    left = dilation + col_off * dilation
    return padded[top:top + GRID_ROWS, left:left + GRID_COLUMNS]

def unfold_patches(weather_field, dilation, sign):
    pieces = []
    for row_off in (-1, 0, 1):
        for col_off in (-1, 0, 1):
            pieces.append(shifted(weather_field, sign * row_off, sign * col_off, dilation))
    return jnp.concatenate(pieces, axis=-1).reshape(GRID_ROWS * GRID_COLUMNS, 9 * CHANNEL_COUNT)

def reference(inputs, lead_ids, film, flat_weights, cotangent):
    highest = lax.Precision.HIGHEST
    weights = flat_weights.astype(jnp.float32).reshape(2, 3, 3, CHANNEL_COUNT, CHANNEL_COUNT)
    matrix_a = weights[0].reshape(9 * CHANNEL_COUNT, CHANNEL_COUNT)
    matrix_b = weights[1].reshape(9 * CHANNEL_COUNT, CHANNEL_COUNT)
    matrix_t = jnp.transpose(weights[1], (0, 1, 3, 2)).reshape(9 * CHANNEL_COUNT, CHANNEL_COUNT)
    scale = 1.0 / math.sqrt(LEADS * GRID_ROWS * GRID_COLUMNS)

    def one_lead(total, items):
        weather_field, lead, upstream_raw = items
        film_row = lax.dynamic_index_in_dim(film, lead, 0, keepdims=False)
        mult_a = 1.0 + film_row[0]
        shift_a = film_row[1]
        mult_b = 1.0 + film_row[2]
        shift_b = film_row[3]
        input_columns = unfold_patches(weather_field, FIRST_DILATION, 1).astype(jnp.float32)
        pre_a = jnp.dot(input_columns, matrix_a, precision=highest) * mult_a + shift_a
        sig_a = jax.nn.sigmoid(pre_a)
        hidden_state = (weather_field.reshape(-1, CHANNEL_COUNT).astype(jnp.float32) + pre_a * sig_a).astype(jnp.bfloat16)
        hidden_columns = unfold_patches(hidden_state.reshape(GRID_ROWS, GRID_COLUMNS, CHANNEL_COUNT), SECOND_DILATION, 1).astype(jnp.float32)
        pre_b = jnp.dot(hidden_columns, matrix_b, precision=highest) * mult_b + shift_b
        sig_b = jax.nn.sigmoid(pre_b)
        result = (hidden_state.astype(jnp.float32) + pre_b * sig_b).astype(jnp.bfloat16)
        upstream = upstream_raw.reshape(-1, CHANNEL_COUNT).astype(jnp.float32)
        second_gradient = (upstream * mult_b * sig_b * (1.0 + pre_b * (1.0 - sig_b))).astype(jnp.bfloat16)
        column_gradient = unfold_patches(second_gradient.reshape(GRID_ROWS, GRID_COLUMNS, CHANNEL_COUNT), SECOND_DILATION, -1).astype(jnp.float32)
        back = upstream + jnp.dot(column_gradient, matrix_t, precision=highest)
        grad_a = (back * mult_a * sig_a * (1.0 + pre_a * (1.0 - sig_a))).astype(jnp.bfloat16)
        blocks_in = input_columns.reshape(N_GY, TILE_R, N_GX, TILE_C, 9 * CHANNEL_COUNT)
        blocks_grad = grad_a.astype(jnp.float32).reshape(N_GY, TILE_R, N_GX, TILE_C, CHANNEL_COUNT)

        def per_row(pair):
            left_part, right_part = pair
            return jnp.einsum('rxck,rxco->ko', left_part, right_part, precision=highest) * scale
        parts = lax.map(per_row, (blocks_in, blocks_grad))
        return (total + lax.optimization_barrier(jnp.sum(parts, axis=0)), result.reshape(GRID_ROWS, GRID_COLUMNS, CHANNEL_COUNT))
    total, results = lax.scan(one_lead, jnp.zeros((9 * CHANNEL_COUNT, CHANNEL_COUNT), jnp.float32), (inputs, lead_ids, cotangent))
    return (results, total.reshape(-1))
```

```python
import math

import jax
import jax.numpy as jnp
import numpy as np
from jax import lax
from jax.experimental import pallas as pl
from jax.experimental.pallas import tpu as pltpu
from jax.sharding import PartitionSpec as P

FIRST_DILATION = 64
SECOND_DILATION = 128
AXES = ("lead", "gy", "gx")


def passed_along(value, axis, steps):
    count = lax.axis_size(axis)
    leading, last = (max(0, -steps), min(count, count - steps))
    return lax.ppermute(value, axis, [(source, source + steps) for source in range(leading, last)])


def shortened(array):
    return jax.tree.map(lambda a: a.astype(jnp.bfloat16) if a.dtype == jnp.float32 else a, array)


def adjacent_cells(weather_field, row_step, col_step):
    row_list = [-1, 0, 1]
    col_list = [-1, 0, 1] if col_step < lax.axis_size("gx") else [0]
    taps = []
    stacked = jnp.stack(
        [
            (
                weather_field
                if row_off == 0
                else passed_along(weather_field, "gy", -row_off * row_step)
            )
            for row_off in row_list
        ]
    )
    columns = [
        (
            stacked
            if col_off == 0
            else passed_along(shortened(stacked), "gx", -col_off * col_step).astype(stacked.dtype)
        )
        for col_off in col_list
    ]
    for col_off in col_list:
        for row_off in row_list:
            taps.append(
                (row_off, col_off, columns[col_list.index(col_off)][row_list.index(row_off)])
            )
    return taps


def lower(taps, weight_four, flipped):
    patch_width = weight_four.shape[-1]
    cols = jnp.concatenate(
        [piece.reshape(-1, patch_width) for row_off, col_off, piece in taps], axis=1
    )
    blocks = []
    for row_off, col_off, piece in taps:
        if flipped:
            blocks.append(weight_four[1 - row_off, 1 - col_off].T)
        else:
            blocks.append(weight_four[row_off + 1, col_off + 1])
    return (cols, jnp.concatenate(blocks, axis=0))


def general_shards(inputs, lead_ids, film, flat_weights, cotangent):
    tile_row_count, tile_column_count, patch_width = (
        inputs.shape[1],
        inputs.shape[2],
        inputs.shape[3],
    )
    gathered = lax.all_gather(flat_weights, AXES, axis=1, tiled=True)
    weight_a = gathered[0].reshape(3, 3, patch_width, patch_width)
    weight_b = gathered[1].reshape(3, 3, patch_width, patch_width)
    film_row = lax.dynamic_index_in_dim(film, lead_ids[0], 0, keepdims=False)
    mult_a = 1.0 + film_row[0]
    shift_a = film_row[1]
    mult_b = 1.0 + film_row[2]
    shift_b = film_row[3]
    weather_field = inputs[0]
    input_kernel_taps = adjacent_cells(
        weather_field, FIRST_DILATION // tile_row_count, FIRST_DILATION // tile_column_count
    )
    input_columns, matrix_a = lower(input_kernel_taps, weight_a, False)
    pre_a = jnp.dot(input_columns, matrix_a, preferred_element_type=jnp.float32) * mult_a + shift_a
    sig_a = jax.nn.sigmoid(pre_a)
    hidden_state = (
        weather_field.reshape(-1, patch_width).astype(jnp.float32) + pre_a * sig_a
    ).astype(jnp.bfloat16)
    taps_hidden = adjacent_cells(
        hidden_state.reshape(tile_row_count, tile_column_count, patch_width),
        SECOND_DILATION // tile_row_count,
        SECOND_DILATION // tile_column_count,
    )
    hidden_columns, matrix_b = lower(taps_hidden, weight_b, False)
    pre_b = jnp.dot(hidden_columns, matrix_b, preferred_element_type=jnp.float32) * mult_b + shift_b
    sig_b = jax.nn.sigmoid(pre_b)
    outputs = (hidden_state.astype(jnp.float32) + pre_b * sig_b).astype(jnp.bfloat16)
    upstream = cotangent[0].reshape(-1, patch_width).astype(jnp.float32)
    second_gradient = (upstream * mult_b * sig_b * (1.0 + pre_b * (1.0 - sig_b))).astype(
        jnp.bfloat16
    )
    taps_grad = adjacent_cells(
        second_gradient.reshape(tile_row_count, tile_column_count, patch_width),
        SECOND_DILATION // tile_row_count,
        SECOND_DILATION // tile_column_count,
    )
    column_gradient, matrix_t = lower(taps_grad, weight_b, True)
    back = upstream + jnp.dot(column_gradient, matrix_t, preferred_element_type=jnp.float32)
    grad_a = (back * mult_a * sig_a * (1.0 + pre_a * (1.0 - sig_a))).astype(jnp.bfloat16)
    scale = 1.0 / math.sqrt(lax.axis_size(AXES) * tile_row_count * tile_column_count)
    products = (
        lax.dot_general(
            input_columns, grad_a, (((0,), (0,)), ((), ())), preferred_element_type=jnp.float32
        )
        * scale
    )
    term = jnp.zeros((3, 3, patch_width, patch_width), jnp.float32)
    for number, (row_off, col_off, piece) in enumerate(input_kernel_taps):
        term = term.at[row_off + 1, col_off + 1].set(
            products[number * patch_width : (number + 1) * patch_width]
        )
    flat_term = term.reshape(lax.axis_size(("lead", "gy")), lax.axis_size("gx"), -1)
    partial_sum = lax.psum_scatter(flat_term, "gx", scatter_dimension=1, tiled=True)
    total = lax.psum_scatter(partial_sum, ("lead", "gy"), scatter_dimension=0, tiled=True)
    return (outputs.reshape(inputs.shape), total.reshape(-1))


def fits(mesh, rows, columns):
    size = mesh.shape
    return (
        tuple(mesh.axis_names) == AXES
        and (size["lead"], size["gy"], size["gx"]) == (2, 4, 4)
        and FIRST_DILATION == rows
        and SECOND_DILATION == 2 * rows
        and FIRST_DILATION // columns >= size["gx"]
    )


def pairs(move):
    number = lambda x, y, c, z: x * 16 + (2 * y + c) * 4 + z
    return [
        (number(x, y, c, z), number(*move(x, y, c, z)))
        for x in range(2)
        for y in range(2)
        for c in range(2)
        for z in range(4)
    ]


def moved(value, dx=0, dy=0, dc=0, dz=0):
    return lax.ppermute(
        value, AXES, pairs(lambda x, y, c, z: (x ^ dx, y ^ dy, c ^ dc, z ^ dz))
    )


CORE_GROUPS = [
    [x * 16 + (2 * y + c) * 4 + z for x in range(2) for y in range(2) for z in range(4)]
    for c in range(2)
]


def used_rows(width, shard_rows):
    found = []
    for block in range(3):
        start = (3 * block + 1) * width
        row = start
        while row < start + width:
            shard = row // shard_rows
            stop = min((shard + 1) * shard_rows, start + width)
            place = (shard // 16, shard // 8 % 2, shard // 4 % 2, shard % 4)
            found.append((*place, row - shard * shard_rows, stop - row, block * width + row - start))
            row = stop
    return found


def main_kernel(
    pieces,
    scale,
    where_ref,
    mine_x,
    other_x,
    mine_ct,
    other_ct,
    near_x0,
    near_x1,
    lane_own,
    lane_other,
    film_ref,
    out_keep,
    out_send,
    grad_keep,
    grad_send,
    weights,
    around,
    total,
):
    x, y, c, z = (where_ref[i] for i in range(4))
    width = film_ref.shape[1]
    half = mine_x.shape[0]
    f32, bf16 = jnp.float32, jnp.bfloat16

    for cx, cy, cc, cz, first, count, row in pieces:
        place = (cx ^ x) + 2 * (cy ^ y)
        for k in range(2):
            own = lane_own[place, cz ^ z, k].astype(f32)
            weights[k, c, row : row + count, :] = own[first : first + count]
            oth = lane_other[place, cz ^ z, k].astype(f32)
            weights[k, 1 - c, row : row + count, :] = oth[first : first + count]

    def block(k, number):
        rows = slice(number * width, (number + 1) * width)
        return jnp.concatenate([weights[k, 0, rows, :], weights[k, 1, rows, :]], axis=1).astype(
            bf16
        )

    first_half = y == 0
    lo = jnp.where(first_half, mine_x[...], other_x[...])
    hi = jnp.where(first_half, other_x[...], mine_x[...])
    mid = jnp.concatenate([lo, hi], axis=0)
    around[0] = jnp.zeros_like(lo)
    around[3] = jnp.zeros_like(lo)
    around[1] = jnp.where(first_half, near_x0[...], near_x1[...])
    around[2] = jnp.where(first_half, near_x1[...], near_x0[...])
    above = jnp.concatenate([around[c], around[c + 1]], axis=0)
    below = jnp.concatenate([around[c + 1], around[c + 2]], axis=0)
    dot = lambda a, b: jnp.dot(a, b, preferred_element_type=f32)
    dot_t = lambda a, b: lax.dot_general(a, b, (((1,), (1,)), ((), ())), preferred_element_type=f32)
    t_dot = lambda a, b: lax.dot_general(a, b, (((0,), (0,)), ((), ())), preferred_element_type=f32)

    mult_a = 1.0 + film_ref[0:1, :]
    shift_a = film_ref[1:2, :]
    mult_b = 1.0 + film_ref[2:3, :]
    shift_b = film_ref[3:4, :]
    conv_a = dot(above, block(0, 0)) + dot(mid, block(0, 1)) + dot(below, block(0, 2))
    pre_a = conv_a * mult_a + shift_a
    sig_a = jax.nn.sigmoid(pre_a)
    hidden = (mid.astype(f32) + pre_a * sig_a).astype(bf16)

    up, centre, down = block(1, 0), block(1, 1), block(1, 2)
    straight = dot(hidden, centre)
    across = jnp.concatenate([dot(hidden[half:], down), dot(hidden[:half], up)], axis=0)
    pre_b = (straight + across) * mult_b + shift_b
    sig_b = jax.nn.sigmoid(pre_b)
    result = (hidden.astype(f32) + pre_b * sig_b).astype(bf16)
    out_keep[...] = jnp.where(first_half, result[:half], result[half:])
    out_send[...] = jnp.where(first_half, result[half:], result[:half])

    ct_lo = jnp.where(first_half, mine_ct[...], other_ct[...])
    ct_hi = jnp.where(first_half, other_ct[...], mine_ct[...])
    upstream = jnp.concatenate([ct_lo, ct_hi], axis=0).astype(f32)
    grad_b = (upstream * mult_b * sig_b * (1.0 + pre_b * (1.0 - sig_b))).astype(bf16)
    back = upstream + dot_t(grad_b, centre)
    back = back + jnp.concatenate([dot_t(grad_b[half:], up), dot_t(grad_b[:half], down)], axis=0)
    grad_a = (back * mult_a * sig_a * (1.0 + pre_a * (1.0 - sig_a))).astype(bf16)

    lane = width // 2
    for number, rows in enumerate((above, mid, below)):
        product = t_dot(rows, grad_a) * scale
        total[0, number * width : (number + 1) * width, :] = product[:, :lane]
        total[1, number * width : (number + 1) * width, :] = product[:, lane:]
    grad_keep[...] = jnp.zeros_like(grad_keep)
    grad_send[...] = jnp.zeros_like(grad_send)
    for cx, cy, cc, cz, first, count, row in pieces:
        chip = cx * 8 + cy * 4 + cz
        grad_keep[chip, first : first + count, :] = total[c, row : row + count, :]
        grad_send[chip, first : first + count, :] = total[1 - c, row : row + count, :]


def last_kernel(where_ref, own_ref, other_ref, out_ref):
    c, low = where_ref[2], where_ref[4]
    rows = own_ref.shape[0]
    row = lax.broadcasted_iota(jnp.int32, own_ref.shape, 0)
    held = jnp.logical_xor(row < low, c == 0)
    own = jnp.where(held, own_ref[...], 0.0)
    other = jnp.where(held, other_ref[...], 0.0)
    out_ref[pl.ds(0, rows, stride=2), :] = jnp.where(c == 0, own, other)
    out_ref[pl.ds(1, rows, stride=2), :] = jnp.where(c == 0, other, own)


def row_shards(inputs, lead_ids, film, flat_weights, cotangent):
    rows, columns, width = inputs.shape[1:]
    half = rows // 2 * columns
    lane = width // 2
    shard_rows = flat_weights.shape[1] // width
    x, gy, z = (lax.axis_index(axis) for axis in AXES)
    y, c = gy // 2, gy % 2
    pieces = used_rows(width, shard_rows)

    low = jnp.where(
        x == 0,
        jnp.where((y == 0) & (z == 3), 40, shard_rows),
        jnp.where((y == 1) & (z == 0), 40, 0),
    )
    where = jnp.stack([x, y, c, z, low]).astype(jnp.int32)

    shard = flat_weights.reshape(2, shard_rows, width)
    left, right = shard[:, :, :lane], shard[:, :, lane:]
    near = moved(jnp.where(c == 0, right, left), dc=1)
    row = lax.broadcasted_iota(jnp.int32, near.shape, 1)
    piece = jnp.where((row < low) == (c == 1), jnp.where(c == 0, left, right), near)
    line = jnp.stack([piece, moved(piece, dz=1), moved(piece, dz=2), moved(piece, dz=3)])
    plane = jnp.stack([line, moved(line, dx=1), moved(line, dy=1), moved(line, dx=1, dy=1)])
    plane_near = moved(plane, dc=1)

    halves_x = inputs.reshape(2, half, width)
    halves_ct = cotangent.reshape(2, half, width)
    pick = lambda halves, number: lax.dynamic_index_in_dim(halves, number, 0, keepdims=False)
    mine_x, mine_ct = pick(halves_x, y), pick(halves_ct, y)
    other_x = moved(pick(halves_x, 1 - y), dy=1)
    other_ct = moved(pick(halves_ct, 1 - y), dy=1)
    near_x0 = moved(mine_x, dc=1)
    near_x1 = moved(other_x, dc=1)
    film_row = lax.dynamic_index_in_dim(film, lead_ids[0], 0, keepdims=False)

    scale = 1.0 / math.sqrt(lax.axis_size(AXES) * rows * columns)
    vmem = pl.BlockSpec(memory_space=pltpu.VMEM)
    smem = pl.BlockSpec(memory_space=pltpu.SMEM)
    chips = 16
    out_keep, out_send, grad_keep, grad_send = pl.pallas_call(
        lambda *refs: main_kernel(pieces, scale, *refs),
        out_shape=(
            jax.ShapeDtypeStruct((half, width), jnp.bfloat16),
            jax.ShapeDtypeStruct((half, width), jnp.bfloat16),
            jax.ShapeDtypeStruct((chips, shard_rows, lane), jnp.float32),
            jax.ShapeDtypeStruct((chips, shard_rows, lane), jnp.float32),
        ),
        in_specs=[smem] + [vmem] * 9,
        out_specs=(vmem,) * 4,
        scratch_shapes=[
            pltpu.VMEM((2, 2, 3 * width, lane), jnp.float32),
            pltpu.VMEM((4, half, width), jnp.bfloat16),
            pltpu.VMEM((2, 3 * width, lane), jnp.float32),
        ],
        compiler_params=pltpu.CompilerParams(vmem_limit_bytes=40 * 1024 * 1024),
        name="blocks",
    )(where, mine_x, other_x, mine_ct, other_ct, near_x0, near_x1, plane, plane_near, film_row)

    other_out = moved(out_send, dy=1)
    first = jnp.where(y == 0, out_keep, other_out)
    second = jnp.where(y == 0, other_out, out_keep)
    outputs = jnp.stack([first, second]).reshape(inputs.shape)

    chip_term = (grad_keep + moved(grad_send, dc=1)).astype(jnp.bfloat16)
    terms = lax.all_to_all(chip_term, AXES, 0, 0, axis_index_groups=CORE_GROUPS)
    lane_sum = jnp.sum(terms.astype(jnp.float32), axis=0)
    total = pl.pallas_call(
        last_kernel,
        out_shape=jax.ShapeDtypeStruct((2 * shard_rows, lane), jnp.float32),
        in_specs=[smem, vmem, vmem],
        out_specs=vmem,
        name="total",
    )(where, lane_sum, moved(lane_sum, dc=1))
    return (outputs, total.reshape(-1))


def solution(mesh):
    def whole(inputs, lead_ids, film, flat_weights, cotangent):
        size = mesh.shape
        rows, columns = inputs.shape[1] // size["gy"], inputs.shape[2] // size["gx"]
        plan = row_shards if fits(mesh, rows, columns) else general_shards
        return jax.shard_map(
            plan,
            mesh=mesh,
            in_specs=(
                P("lead", "gy", "gx", None),
                P("lead"),
                P(),
                P(None, AXES),
                P("lead", "gy", "gx", None),
            ),
            out_specs=(P("lead", "gy", "gx", None), P(AXES)),
            check_vma=False,
        )(inputs, lead_ids, film, flat_weights, cotangent)

    return whole
```

```python
import math

import jax
import jax.numpy as jnp
from jax import lax
from jax.experimental import pallas as pl
from jax.experimental.pallas import tpu as pltpu
from jax.sharding import PartitionSpec as P

FIRST_DILATION = 64
SECOND_DILATION = 128
AXES = ("lead", "gy", "gx")


def passed_along(value, axis, steps):
    count = lax.axis_size(axis)
    leading, last = (max(0, -steps), min(count, count - steps))
    return lax.ppermute(value, axis, [(source, source + steps) for source in range(leading, last)])


def shortened(array):
    return jax.tree.map(lambda a: a.astype(jnp.bfloat16) if a.dtype == jnp.float32 else a, array)


def adjacent_cells(weather_field, row_step, col_step):
    row_list = [-1, 0, 1]
    col_list = [-1, 0, 1] if col_step < lax.axis_size("gx") else [0]
    taps = []
    stacked = jnp.stack(
        [
            (
                weather_field
                if row_off == 0
                else passed_along(weather_field, "gy", -row_off * row_step)
            )
            for row_off in row_list
        ]
    )
    columns = [
        (
            stacked
            if col_off == 0
            else passed_along(shortened(stacked), "gx", -col_off * col_step).astype(stacked.dtype)
        )
        for col_off in col_list
    ]
    for col_off in col_list:
        for row_off in row_list:
            taps.append(
                (row_off, col_off, columns[col_list.index(col_off)][row_list.index(row_off)])
            )
    return taps


def lower(taps, weight_four, flipped):
    patch_width = weight_four.shape[-1]
    cols = jnp.concatenate(
        [piece.reshape(-1, patch_width) for row_off, col_off, piece in taps], axis=1
    )
    blocks = []
    for row_off, col_off, piece in taps:
        if flipped:
            blocks.append(weight_four[1 - row_off, 1 - col_off].T)
        else:
            blocks.append(weight_four[row_off + 1, col_off + 1])
    return (cols, jnp.concatenate(blocks, axis=0))


def general_shards(inputs, lead_ids, film, flat_weights, cotangent):
    tile_row_count, tile_column_count, patch_width = (
        inputs.shape[1],
        inputs.shape[2],
        inputs.shape[3],
    )
    gathered = lax.all_gather(flat_weights, AXES, axis=1, tiled=True)
    weight_a = gathered[0].reshape(3, 3, patch_width, patch_width)
    weight_b = gathered[1].reshape(3, 3, patch_width, patch_width)
    film_row = lax.dynamic_index_in_dim(film, lead_ids[0], 0, keepdims=False)
    mult_a = 1.0 + film_row[0]
    shift_a = film_row[1]
    mult_b = 1.0 + film_row[2]
    shift_b = film_row[3]
    weather_field = inputs[0]
    input_kernel_taps = adjacent_cells(
        weather_field, FIRST_DILATION // tile_row_count, FIRST_DILATION // tile_column_count
    )
    input_columns, matrix_a = lower(input_kernel_taps, weight_a, False)
    pre_a = jnp.dot(input_columns, matrix_a, preferred_element_type=jnp.float32) * mult_a + shift_a
    sig_a = jax.nn.sigmoid(pre_a)
    hidden_state = (
        weather_field.reshape(-1, patch_width).astype(jnp.float32) + pre_a * sig_a
    ).astype(jnp.bfloat16)
    taps_hidden = adjacent_cells(
        hidden_state.reshape(tile_row_count, tile_column_count, patch_width),
        SECOND_DILATION // tile_row_count,
        SECOND_DILATION // tile_column_count,
    )
    hidden_columns, matrix_b = lower(taps_hidden, weight_b, False)
    pre_b = jnp.dot(hidden_columns, matrix_b, preferred_element_type=jnp.float32) * mult_b + shift_b
    sig_b = jax.nn.sigmoid(pre_b)
    outputs = (hidden_state.astype(jnp.float32) + pre_b * sig_b).astype(jnp.bfloat16)
    upstream = cotangent[0].reshape(-1, patch_width).astype(jnp.float32)
    second_gradient = (upstream * mult_b * sig_b * (1.0 + pre_b * (1.0 - sig_b))).astype(
        jnp.bfloat16
    )
    taps_grad = adjacent_cells(
        second_gradient.reshape(tile_row_count, tile_column_count, patch_width),
        SECOND_DILATION // tile_row_count,
        SECOND_DILATION // tile_column_count,
    )
    column_gradient, matrix_t = lower(taps_grad, weight_b, True)
    back = upstream + jnp.dot(column_gradient, matrix_t, preferred_element_type=jnp.float32)
    grad_a = (back * mult_a * sig_a * (1.0 + pre_a * (1.0 - sig_a))).astype(jnp.bfloat16)
    scale = 1.0 / math.sqrt(lax.axis_size(AXES) * tile_row_count * tile_column_count)
    products = (
        lax.dot_general(
            input_columns, grad_a, (((0,), (0,)), ((), ())), preferred_element_type=jnp.float32
        )
        * scale
    )
    term = jnp.zeros((3, 3, patch_width, patch_width), jnp.float32)
    for number, (row_off, col_off, piece) in enumerate(input_kernel_taps):
        term = term.at[row_off + 1, col_off + 1].set(
            products[number * patch_width : (number + 1) * patch_width]
        )
    flat_term = term.reshape(lax.axis_size(("lead", "gy")), lax.axis_size("gx"), -1)
    partial_sum = lax.psum_scatter(flat_term, "gx", scatter_dimension=1, tiled=True)
    total = lax.psum_scatter(partial_sum, ("lead", "gy"), scatter_dimension=0, tiled=True)
    return (outputs.reshape(inputs.shape), total.reshape(-1))


def fits(mesh, rows, columns):
    size = mesh.shape
    return (
        tuple(mesh.axis_names) == AXES
        and (size["lead"], size["gy"], size["gx"]) == (2, 4, 4)
        and FIRST_DILATION == rows
        and SECOND_DILATION == 2 * rows
        and FIRST_DILATION // columns >= size["gx"]
    )


def pairs(move):
    number = lambda x, y, c, z: x * 16 + (2 * y + c) * 4 + z
    return [
        (number(x, y, c, z), number(*move(x, y, c, z)))
        for x in range(2)
        for y in range(2)
        for c in range(2)
        for z in range(4)
    ]


def moved(value, dx=0, dy=0, dc=0, dz=0):
    return lax.ppermute(
        value, AXES, pairs(lambda x, y, c, z: (x ^ dx, y ^ dy, c ^ dc, z ^ dz))
    )


Z_ORDER = (3, 2, 1)
PLANE_ORDER = ((1, 1), (1, 0), (0, 1))


def place():
    x, gy, z = (lax.axis_index(axis) for axis in AXES)
    return x, gy // 2, gy % 2, z


def used_rows(width, shard_rows):
    found = []
    for block in range(3):
        start = (3 * block + 1) * width
        row = start
        while row < start + width:
            shard = row // shard_rows
            stop = min((shard + 1) * shard_rows, start + width)
            place = (shard // 16, shard // 8 % 2, shard // 4 % 2, shard % 4)
            found.append((*place, row - shard * shard_rows, stop - row, block * width + row - start))
            row = stop
    return found


def chosen(table, here, otherwise):
    value = otherwise
    for key, entry in table.items():
        if entry != otherwise:
            match = here[0] == key[0]
            for mine, wanted in zip(here[1:], key[1:]):
                match = match & (mine == wanted)
            value = jnp.where(match, entry, value)
    return value


class Layout:
    def __init__(self, width, shard_rows):
        self.pieces = used_rows(width, shard_rows)
        self.start, self.count, self.base, self.first, self.stop = {}, {}, {}, {}, {}
        for cx, cy, cc, cz, first, count, row in self.pieces:
            self.start[cx, cy] = min(self.start.get((cx, cy), 3 * width), row)
            self.count[cx, cy] = self.count.get((cx, cy), 0) + count
        for cx, cy, cc, cz, first, count, row in self.pieces:
            self.base[cx, cy, cz, cc] = row - self.start[cx, cy] - first
            self.first[cx, cy, cz, cc] = first
            self.stop[cx, cy, cz, cc] = first + count
        self.low = {
            key[:3]: stop for key, stop in self.stop.items() if key[3] == 1
        }
        for key, first in self.first.items():
            assert key[3] == 1 or self.low.get(key[:3], 0) <= first
        self.column_rows = max(self.count.values())
        assert all(start + self.column_rows <= 3 * width for start in self.start.values())
        assert len(self.base) == len(self.pieces)


def line_kernel(layout, own_ref, far0_ref, far1_ref, far2_ref, out_ref, total):
    x, y, c, z = place()
    rows = own_ref.shape[1]
    total[...] = jnp.zeros_like(total)
    row = lax.broadcasted_iota(jnp.int32, own_ref.shape[1:], 0)
    for dz, ref in zip((0, *Z_ORDER), (own_ref, far0_ref, far1_ref, far2_ref)):
        for core in range(2):
            here = (x, y, z ^ dz, core)
            first, stop = chosen(layout.first, here, 0), chosen(layout.stop, here, 0)
            base = pl.multiple_of(rows + chosen(layout.base, here, -rows), 8)
            used = (row >= first) & (row < stop)
            for k in range(2):
                value = jnp.where(used, ref[k].astype(jnp.float32), 0.0)
                total[k, pl.ds(base, rows), :] += value
    out_ref[...] = total[:, rows : rows + out_ref.shape[1], :].astype(out_ref.dtype)


def slot(dx, dy):
    found = 0
    for number, (to_x, to_y) in enumerate(PLANE_ORDER):
        found = jnp.where((dx == to_x) & (dy == to_y), number + 1, found)
    return found


def matrix(layout, own_ref, near_ref):
    x, y, c, z = place()
    halves = []
    for ref in (own_ref, near_ref):
        parts = [
            ref[slot(cx ^ x, cy ^ y)][: layout.count[cx, cy]]
            for cx, cy in sorted(layout.start, key=layout.start.get)
        ]
        halves.append(jnp.concatenate(parts, axis=0))
    own, near = halves
    return jnp.concatenate([jnp.where(c == 0, own, near), jnp.where(c == 0, near, own)], axis=1)


def dot(a, b, dims=((1,), (0,))):
    return lax.dot_general(a, b, (dims, ((), ())), preferred_element_type=jnp.float32)


def first_kernel(
    layout, mine_ref, other_ref, near0_ref, near1_ref, own_w, near_w, film_ref,
    field_ref, pre_ref, hidden_ref,
):
    x, y, c, z = place()
    half, width = mine_ref.shape
    near0, near1 = near0_ref[...], near1_ref[...]
    mine, other = mine_ref[...], other_ref[0]
    lo, hi = jnp.where(y == 0, mine, other), jnp.where(y == 0, other, mine)
    near_lo, near_hi = jnp.where(y == 0, near0, near1), jnp.where(y == 0, near1, near0)
    field_ref[0] = jnp.zeros_like(lo)
    field_ref[1] = jnp.where(c == 0, lo, near_lo)
    field_ref[2] = jnp.where(c == 0, near_lo, lo)
    field_ref[3] = jnp.where(c == 0, hi, near_hi)
    field_ref[4] = jnp.where(c == 0, near_hi, hi)
    field_ref[5] = jnp.zeros_like(lo)
    above = jnp.concatenate([field_ref[c], field_ref[c + 2]], axis=0)
    mid = jnp.concatenate([lo, hi], axis=0)
    below = jnp.concatenate([field_ref[c + 2], field_ref[c + 4]], axis=0)
    weight = matrix(layout, own_w, near_w)
    conv = dot(above, weight[:width]) + dot(mid, weight[width : 2 * width])
    conv = conv + dot(below, weight[2 * width :])
    pre = conv * (1.0 + film_ref[0:1, :]) + film_ref[1:2, :]
    pre_ref[...] = pre
    hidden_ref[...] = (mid.astype(jnp.float32) + pre * jax.nn.sigmoid(pre)).astype(hidden_ref.dtype)


def second_kernel(
    layout, pre_ref, hidden_ref, mine_ct, other_ref, own_w, near_w, film_ref,
    out_keep, out_send, grad_keep, grad_send,
):
    x, y, c, z = place()
    half, width = mine_ct.shape
    f32, bf16 = jnp.float32, jnp.bfloat16
    lane = width // 2
    mult_a = 1.0 + film_ref[0:1, :]
    mult_b = 1.0 + film_ref[2:3, :]
    weight = matrix(layout, own_w, near_w)
    up, centre, down = weight[:width], weight[width : 2 * width], weight[2 * width :]
    hidden = hidden_ref[...]
    across = jnp.concatenate([dot(hidden[half:], down), dot(hidden[:half], up)], axis=0)
    pre_b = (dot(hidden, centre) + across) * mult_b + film_ref[3:4, :]
    sig_b = jax.nn.sigmoid(pre_b)
    result = (hidden.astype(f32) + pre_b * sig_b).astype(bf16)
    out_keep[...] = jnp.where(y == 0, result[:half], result[half:])
    out_send[...] = jnp.where(y == 0, result[half:], result[:half])
    mine, other = mine_ct[...], other_ref[1]
    lo, hi = jnp.where(y == 0, mine, other), jnp.where(y == 0, other, mine)
    upstream = jnp.concatenate([lo, hi], axis=0).astype(f32)
    grad_b = (upstream * mult_b * sig_b * (1.0 + pre_b * (1.0 - sig_b))).astype(bf16)
    turned = ((1,), (1,))
    back = jnp.concatenate(
        [dot(grad_b[half:], up, turned), dot(grad_b[:half], down, turned)], axis=0
    )
    back = upstream + dot(grad_b, centre, turned) + back
    pre_a = pre_ref[...]
    sig_a = jax.nn.sigmoid(pre_a)
    grad_a = (back * mult_a * sig_a * (1.0 + pre_a * (1.0 - sig_a))).astype(bf16)
    grad_keep[...] = jnp.where(c == 0, grad_a[:, :lane], grad_a[:, lane:])
    grad_send[...] = jnp.where(c == 0, grad_a[:, lane:], grad_a[:, :lane])


def term_kernel(
    layout, scale, field_ref, keep_ref, near_ref, own_ref, far0_ref, far1_ref, far2_ref, total
):
    x, y, c, z = place()
    half, width = field_ref.shape[1:]
    keep, near = keep_ref[...], near_ref[...]
    even, odd = jnp.where(c == 0, keep, near), jnp.where(c == 0, near, keep)
    grad = jnp.concatenate([even[:half], odd[:half], even[half:], odd[half:]], axis=0)
    field = jnp.concatenate([field_ref[tile] for tile in range(1, 5)], axis=0)
    over = ((0,), (0,))
    total[:width, :] = dot(field[: 3 * half], grad[half:], over) * scale
    total[width : 2 * width, :] = dot(field, grad, over) * scale
    total[2 * width :, :] = dot(field[half:], grad[: 3 * half], over) * scale
    rows = own_ref.shape[0]
    for (dx, dy), ref in zip(((0, 0), *PLANE_ORDER), (own_ref, far0_ref, far1_ref, far2_ref)):
        start = pl.multiple_of(chosen(layout.start, (x ^ dx, y ^ dy), 0), 8)
        ref[...] = total[pl.ds(start, rows), :].astype(ref.dtype)


def chip_kernel(layout, own_ref, far0_ref, far1_ref, far2_ref, out0, out1, out2, out3, total):
    x, y, c, z = place()
    f32 = jnp.float32
    rows, lane = own_ref.shape
    piece_rows = out0.shape[0]
    value = own_ref[...]
    for ref in (far0_ref, far1_ref, far2_ref):
        value = value + ref[...].astype(f32)
    row = lax.broadcasted_iota(jnp.int32, value.shape, 0)
    edge = jnp.zeros((piece_rows, lane), f32)
    total[0:piece_rows, :] = edge
    held = row < chosen(layout.count, (x, y), 0)
    total[piece_rows : piece_rows + rows, :] = jnp.where(held, value, 0.0)
    total[piece_rows + rows :, :] = edge
    for dz, ref in zip((0, *Z_ORDER), (out0, out1, out2, out3)):
        ends = []
        for core in range(2):
            base = piece_rows + chosen(layout.base, (x, y, z ^ dz, core), -piece_rows)
            ends.append(total[pl.ds(pl.multiple_of(base, 8), piece_rows), :])
        ref[...] = (ends[0] + ends[1]).astype(ref.dtype)


def last_kernel(layout, own_ref, other_ref, out_ref):
    x, y, c, z = place()
    rows = own_ref.shape[0]
    row = lax.broadcasted_iota(jnp.int32, own_ref.shape, 0)
    held = jnp.logical_xor(row < chosen(layout.low, (x, y, z), 0), c == 0)
    own = jnp.where(held, own_ref[...], 0.0)
    other = jnp.where(held, other_ref[...], 0.0)
    out_ref[pl.ds(0, rows, stride=2), :] = jnp.where(c == 0, own, other)
    out_ref[pl.ds(1, rows, stride=2), :] = jnp.where(c == 0, other, own)


def row_shards(inputs, lead_ids, film, flat_weights, cotangent):
    rows, columns, width = inputs.shape[1:]
    half = rows // 2 * columns
    lane = width // 2
    shard_rows = flat_weights.shape[1] // width
    x, y, c, z = place()
    layout = Layout(width, shard_rows)
    bf16, f32 = jnp.bfloat16, jnp.float32
    shape = jax.ShapeDtypeStruct

    def call(name, body, out_shape, scratch, *operands, space=pltpu.VMEM, mib=16):
        vmem = pl.BlockSpec(memory_space=pltpu.VMEM)
        several = isinstance(out_shape, tuple)
        return pl.pallas_call(
            lambda *refs: body(layout, *refs),
            out_shape=out_shape,
            in_specs=[pl.BlockSpec(memory_space=space)] * len(operands),
            out_specs=(vmem,) * len(out_shape) if several else vmem,
            scratch_shapes=scratch,
            compiler_params=pltpu.CompilerParams(vmem_limit_bytes=mib * 1024 * 1024),
            name=name,
        )(*operands)

    shard = flat_weights.reshape(2, shard_rows, width)
    left, right = shard[:, :, :lane], shard[:, :, lane:]
    near = moved(jnp.where(c == 0, right, left), dc=1)
    row = lax.broadcasted_iota(jnp.int32, near.shape, 1)
    from_one = row < chosen(layout.low, (x, y, z), 0)
    piece = jnp.where(from_one == (c == 1), jnp.where(c == 0, left, right), near)

    halves_x, halves_ct = (array.reshape(2, half, width) for array in (inputs, cotangent))
    pick = lambda halves, number: lax.dynamic_index_in_dim(halves, number, 0, keepdims=False)
    other = moved(jnp.stack([pick(halves_x, 1 - y), pick(halves_ct, 1 - y)]), dy=1)
    line = [piece, *(moved(piece, dz=dz) for dz in Z_ORDER)]
    *line, other, halves_x, halves_ct, film = lax.optimization_barrier(
        (*line, other, halves_x, halves_ct, film)
    )
    mine_x, mine_ct = pick(halves_x, y), pick(halves_ct, y)
    film_row = lax.dynamic_index_in_dim(film, lead_ids[0], 0, keepdims=False)
    near_x0 = moved(mine_x, dc=1)
    line = call(
        "line",
        line_kernel,
        shape((2, layout.column_rows, lane), bf16),
        [pltpu.VMEM((2, layout.column_rows + 2 * shard_rows, lane), f32)],
        *line,
    )
    near_x1 = moved(other[0], dc=1)
    plane = [line, *(moved(line, dx=dx, dy=dy) for dx, dy in PLANE_ORDER)]
    *plane, near_x0, near_x1, mine_x, mine_ct, film_row = lax.optimization_barrier(
        (*plane, near_x0, near_x1, mine_x, mine_ct, film_row)
    )
    own_a, own_b = (jnp.stack([column[k] for column in plane]) for k in range(2))
    near_a, near_b = moved(own_a, dc=1), moved(own_b, dc=1)

    field, pre_a, hidden = call(
        "block_one",
        first_kernel,
        (shape((6, half, width), bf16), shape((2 * half, width), f32), shape((2 * half, width), bf16)),
        [],
        *(mine_x, other, near_x0, near_x1, own_a, near_a, film_row),
    )
    out_keep, out_send, grad_keep, grad_send = call(
        "block_two",
        second_kernel,
        (shape((half, width), bf16),) * 2 + (shape((2 * half, lane), bf16),) * 2,
        [],
        *(pre_a, hidden, mine_ct, other, own_b, near_b, film_row),
    )

    scale = 1.0 / math.sqrt(lax.axis_size(AXES) * rows * columns)
    column = call(
        "terms",
        lambda layout, *refs: term_kernel(layout, scale, *refs),
        (shape((layout.column_rows, lane), f32),) + (shape((layout.column_rows, lane), bf16),) * 3,
        [pltpu.VMEM((3 * width, lane), f32)],
        *(field, grad_keep, moved(grad_send, dc=1)),
    )
    other_out = moved(out_send, dy=1)
    column = [column[0], *(moved(term, dx=dx, dy=dy) for term, (dx, dy) in zip(column[1:], PLANE_ORDER))]
    chip = call(
        "chips",
        chip_kernel,
        (shape((shard_rows, lane), f32),) + (shape((shard_rows, lane), bf16),) * 3,
        [pltpu.VMEM((layout.column_rows + 2 * shard_rows, lane), f32)],
        *column,
    )
    lane_sum = chip[0]
    for term, dz in reversed(list(zip(chip[1:], Z_ORDER))):
        lane_sum = lane_sum + moved(term, dz=dz).astype(f32)

    first = jnp.where(y == 0, out_keep, other_out)
    second = jnp.where(y == 0, other_out, out_keep)
    outputs = jnp.stack([first, second]).reshape(inputs.shape)

    total = call(
        "total",
        last_kernel,
        shape((2 * shard_rows, lane), f32),
        [],
        *(lane_sum, moved(lane_sum, dc=1)),
    )
    return (outputs, total.reshape(-1))


def solution(mesh):
    def whole(inputs, lead_ids, film, flat_weights, cotangent):
        size = mesh.shape
        rows, columns = inputs.shape[1] // size["gy"], inputs.shape[2] // size["gx"]
        plan = row_shards if fits(mesh, rows, columns) else general_shards
        return jax.shard_map(
            plan,
            mesh=mesh,
            in_specs=(
                P("lead", "gy", "gx", None),
                P("lead"),
                P(),
                P(None, AXES),
                P("lead", "gy", "gx", None),
            ),
            out_specs=(P("lead", "gy", "gx", None), P(AXES)),
            check_vma=False,
        )(inputs, lead_ids, film, flat_weights, cotangent)

    return whole
```

```python
import math

import jax
import jax.numpy as jnp
from jax import lax
from jax.experimental import pallas as pl
from jax.experimental.pallas import tpu as pltpu
from jax.sharding import PartitionSpec as P

FIRST_DILATION = 64
SECOND_DILATION = 128
AXES = ("lead", "gy", "gx")


def passed_along(value, axis, steps):
    count = lax.axis_size(axis)
    leading, last = (max(0, -steps), min(count, count - steps))
    return lax.ppermute(value, axis, [(source, source + steps) for source in range(leading, last)])


def shortened(array):
    return jax.tree.map(lambda a: a.astype(jnp.bfloat16) if a.dtype == jnp.float32 else a, array)


def adjacent_cells(weather_field, row_step, col_step):
    row_list = [-1, 0, 1]
    col_list = [-1, 0, 1] if col_step < lax.axis_size("gx") else [0]
    taps = []
    stacked = jnp.stack(
        [
            (
                weather_field
                if row_off == 0
                else passed_along(weather_field, "gy", -row_off * row_step)
            )
            for row_off in row_list
        ]
    )
    columns = [
        (
            stacked
            if col_off == 0
            else passed_along(shortened(stacked), "gx", -col_off * col_step).astype(stacked.dtype)
        )
        for col_off in col_list
    ]
    for col_off in col_list:
        for row_off in row_list:
            taps.append(
                (row_off, col_off, columns[col_list.index(col_off)][row_list.index(row_off)])
            )
    return taps


def lower(taps, weight_four, flipped):
    patch_width = weight_four.shape[-1]
    cols = jnp.concatenate(
        [piece.reshape(-1, patch_width) for row_off, col_off, piece in taps], axis=1
    )
    blocks = []
    for row_off, col_off, piece in taps:
        if flipped:
            blocks.append(weight_four[1 - row_off, 1 - col_off].T)
        else:
            blocks.append(weight_four[row_off + 1, col_off + 1])
    return (cols, jnp.concatenate(blocks, axis=0))


def general_shards(inputs, lead_ids, film, flat_weights, cotangent):
    tile_row_count, tile_column_count, patch_width = (
        inputs.shape[1],
        inputs.shape[2],
        inputs.shape[3],
    )
    gathered = lax.all_gather(flat_weights, AXES, axis=1, tiled=True)
    weight_a = gathered[0].reshape(3, 3, patch_width, patch_width)
    weight_b = gathered[1].reshape(3, 3, patch_width, patch_width)
    film_row = lax.dynamic_index_in_dim(film, lead_ids[0], 0, keepdims=False)
    mult_a = 1.0 + film_row[0]
    shift_a = film_row[1]
    mult_b = 1.0 + film_row[2]
    shift_b = film_row[3]
    weather_field = inputs[0]
    input_kernel_taps = adjacent_cells(
        weather_field, FIRST_DILATION // tile_row_count, FIRST_DILATION // tile_column_count
    )
    input_columns, matrix_a = lower(input_kernel_taps, weight_a, False)
    pre_a = jnp.dot(input_columns, matrix_a, preferred_element_type=jnp.float32) * mult_a + shift_a
    sig_a = jax.nn.sigmoid(pre_a)
    hidden_state = (
        weather_field.reshape(-1, patch_width).astype(jnp.float32) + pre_a * sig_a
    ).astype(jnp.bfloat16)
    taps_hidden = adjacent_cells(
        hidden_state.reshape(tile_row_count, tile_column_count, patch_width),
        SECOND_DILATION // tile_row_count,
        SECOND_DILATION // tile_column_count,
    )
    hidden_columns, matrix_b = lower(taps_hidden, weight_b, False)
    pre_b = jnp.dot(hidden_columns, matrix_b, preferred_element_type=jnp.float32) * mult_b + shift_b
    sig_b = jax.nn.sigmoid(pre_b)
    outputs = (hidden_state.astype(jnp.float32) + pre_b * sig_b).astype(jnp.bfloat16)
    upstream = cotangent[0].reshape(-1, patch_width).astype(jnp.float32)
    second_gradient = (upstream * mult_b * sig_b * (1.0 + pre_b * (1.0 - sig_b))).astype(
        jnp.bfloat16
    )
    taps_grad = adjacent_cells(
        second_gradient.reshape(tile_row_count, tile_column_count, patch_width),
        SECOND_DILATION // tile_row_count,
        SECOND_DILATION // tile_column_count,
    )
    column_gradient, matrix_t = lower(taps_grad, weight_b, True)
    back = upstream + jnp.dot(column_gradient, matrix_t, preferred_element_type=jnp.float32)
    grad_a = (back * mult_a * sig_a * (1.0 + pre_a * (1.0 - sig_a))).astype(jnp.bfloat16)
    scale = 1.0 / math.sqrt(lax.axis_size(AXES) * tile_row_count * tile_column_count)
    products = (
        lax.dot_general(
            input_columns, grad_a, (((0,), (0,)), ((), ())), preferred_element_type=jnp.float32
        )
        * scale
    )
    term = jnp.zeros((3, 3, patch_width, patch_width), jnp.float32)
    for number, (row_off, col_off, piece) in enumerate(input_kernel_taps):
        term = term.at[row_off + 1, col_off + 1].set(
            products[number * patch_width : (number + 1) * patch_width]
        )
    flat_term = term.reshape(lax.axis_size(("lead", "gy")), lax.axis_size("gx"), -1)
    partial_sum = lax.psum_scatter(flat_term, "gx", scatter_dimension=1, tiled=True)
    total = lax.psum_scatter(partial_sum, ("lead", "gy"), scatter_dimension=0, tiled=True)
    return (outputs.reshape(inputs.shape), total.reshape(-1))


def fits(mesh, rows, columns):
    size = mesh.shape
    return (
        tuple(mesh.axis_names) == AXES
        and (size["lead"], size["gy"], size["gx"]) == (2, 4, 4)
        and FIRST_DILATION == rows
        and SECOND_DILATION == 2 * rows
        and FIRST_DILATION // columns >= size["gx"]
    )


def pairs(move):
    number = lambda x, y, c, z: x * 16 + (2 * y + c) * 4 + z
    return [
        (number(x, y, c, z), number(*move(x, y, c, z)))
        for x in range(2)
        for y in range(2)
        for c in range(2)
        for z in range(4)
    ]


def moved(value, dx=0, dy=0, dc=0, dz=0):
    return lax.ppermute(
        value, AXES, pairs(lambda x, y, c, z: (x ^ dx, y ^ dy, c ^ dc, z ^ dz))
    )


Z_ORDER = (3, 2, 1)
PLANE_ORDER = ((1, 1), (1, 0), (0, 1))


def place():
    x, gy, z = (lax.axis_index(axis) for axis in AXES)
    return x, gy // 2, gy % 2, z


def used_rows(width, shard_rows):
    found = []
    for block in range(3):
        start = (3 * block + 1) * width
        row = start
        while row < start + width:
            shard = row // shard_rows
            stop = min((shard + 1) * shard_rows, start + width)
            place = (shard // 16, shard // 8 % 2, shard // 4 % 2, shard % 4)
            found.append((*place, row - shard * shard_rows, stop - row, block * width + row - start))
            row = stop
    return found


def chosen(table, here, otherwise):
    value = otherwise
    for key, entry in table.items():
        if entry != otherwise:
            match = here[0] == key[0]
            for mine, wanted in zip(here[1:], key[1:]):
                match = match & (mine == wanted)
            value = jnp.where(match, entry, value)
    return value


class Layout:
    def __init__(self, width, shard_rows):
        self.pieces = used_rows(width, shard_rows)
        self.start, self.count, self.base, self.first, self.stop = {}, {}, {}, {}, {}
        for cx, cy, cc, cz, first, count, row in self.pieces:
            self.start[cx, cy] = min(self.start.get((cx, cy), 3 * width), row)
            self.count[cx, cy] = self.count.get((cx, cy), 0) + count
        for cx, cy, cc, cz, first, count, row in self.pieces:
            self.base[cx, cy, cz, cc] = row - self.start[cx, cy] - first
            self.first[cx, cy, cz, cc] = first
            self.stop[cx, cy, cz, cc] = first + count
        self.low = {
            key[:3]: stop for key, stop in self.stop.items() if key[3] == 1
        }
        for key, first in self.first.items():
            assert key[3] == 1 or self.low.get(key[:3], 0) <= first
        self.column_rows = max(self.count.values())
        assert all(start + self.column_rows <= 3 * width for start in self.start.values())
        assert len(self.base) == len(self.pieces)


def line_kernel(layout, own_ref, far0_ref, far1_ref, far2_ref, out_ref, total):
    x, y, c, z = place()
    rows = own_ref.shape[1]
    total[...] = jnp.zeros_like(total)
    row = lax.broadcasted_iota(jnp.int32, own_ref.shape[1:], 0)
    for dz, ref in zip((0, *Z_ORDER), (own_ref, far0_ref, far1_ref, far2_ref)):
        for core in range(2):
            here = (x, y, z ^ dz, core)
            first, stop = chosen(layout.first, here, 0), chosen(layout.stop, here, 0)
            base = pl.multiple_of(rows + chosen(layout.base, here, -rows), 8)
            used = (row >= first) & (row < stop)
            for k in range(2):
                value = jnp.where(used, ref[k].astype(jnp.float32), 0.0)
                total[k, pl.ds(base, rows), :] += value
    out_ref[...] = total[:, rows : rows + out_ref.shape[1], :].astype(out_ref.dtype)


def slot(dx, dy):
    found = 0
    for number, (to_x, to_y) in enumerate(PLANE_ORDER):
        found = jnp.where((dx == to_x) & (dy == to_y), number + 1, found)
    return found


def matrix(layout, own_ref, near_ref):
    x, y, c, z = place()
    halves = []
    for ref in (own_ref, near_ref):
        parts = [
            ref[slot(cx ^ x, cy ^ y)][: layout.count[cx, cy]]
            for cx, cy in sorted(layout.start, key=layout.start.get)
        ]
        halves.append(jnp.concatenate(parts, axis=0))
    own, near = halves
    return jnp.concatenate([jnp.where(c == 0, own, near), jnp.where(c == 0, near, own)], axis=1)


def dot(a, b, dims=((1,), (0,))):
    return lax.dot_general(a, b, (dims, ((), ())), preferred_element_type=jnp.float32)


def first_kernel(
    layout, mine_ref, other_ref, near0_ref, near1_ref, own_w, near_w, film_ref,
    field_ref, pre_ref, hidden_ref,
):
    x, y, c, z = place()
    half, width = mine_ref.shape
    near0, near1 = near0_ref[...], near1_ref[...]
    mine, other = mine_ref[...], other_ref[0]
    lo, hi = jnp.where(y == 0, mine, other), jnp.where(y == 0, other, mine)
    near_lo, near_hi = jnp.where(y == 0, near0, near1), jnp.where(y == 0, near1, near0)
    field_ref[0] = jnp.zeros_like(lo)
    field_ref[1] = jnp.where(c == 0, lo, near_lo)
    field_ref[2] = jnp.where(c == 0, near_lo, lo)
    field_ref[3] = jnp.where(c == 0, hi, near_hi)
    field_ref[4] = jnp.where(c == 0, near_hi, hi)
    field_ref[5] = jnp.zeros_like(lo)
    above = jnp.concatenate([field_ref[c], field_ref[c + 2]], axis=0)
    mid = jnp.concatenate([lo, hi], axis=0)
    below = jnp.concatenate([field_ref[c + 2], field_ref[c + 4]], axis=0)
    weight = matrix(layout, own_w, near_w)
    conv = dot(above, weight[:width]) + dot(mid, weight[width : 2 * width])
    conv = conv + dot(below, weight[2 * width :])
    pre = conv * (1.0 + film_ref[0:1, :]) + film_ref[1:2, :]
    pre_ref[...] = pre
    hidden_ref[...] = (mid.astype(jnp.float32) + pre * jax.nn.sigmoid(pre)).astype(hidden_ref.dtype)


def second_kernel(
    layout, pre_ref, hidden_ref, mine_ct, other_ref, own_w, near_w, film_ref,
    out_keep, out_send, grad_keep, grad_send,
):
    x, y, c, z = place()
    half, width = mine_ct.shape
    f32, bf16 = jnp.float32, jnp.bfloat16
    lane = width // 2
    mult_a = 1.0 + film_ref[0:1, :]
    mult_b = 1.0 + film_ref[2:3, :]
    weight = matrix(layout, own_w, near_w)
    up, centre, down = weight[:width], weight[width : 2 * width], weight[2 * width :]
    hidden = hidden_ref[...]
    across = jnp.concatenate([dot(hidden[half:], down), dot(hidden[:half], up)], axis=0)
    pre_b = (dot(hidden, centre) + across) * mult_b + film_ref[3:4, :]
    sig_b = jax.nn.sigmoid(pre_b)
    result = (hidden.astype(f32) + pre_b * sig_b).astype(bf16)
    out_keep[...] = jnp.where(y == 0, result[:half], result[half:])
    out_send[...] = jnp.where(y == 0, result[half:], result[:half])
    mine, other = mine_ct[...], other_ref[1]
    lo, hi = jnp.where(y == 0, mine, other), jnp.where(y == 0, other, mine)
    upstream = jnp.concatenate([lo, hi], axis=0).astype(f32)
    grad_b = (upstream * mult_b * sig_b * (1.0 + pre_b * (1.0 - sig_b))).astype(bf16)
    turned = ((1,), (1,))
    back = jnp.concatenate(
        [dot(grad_b[half:], up, turned), dot(grad_b[:half], down, turned)], axis=0
    )
    back = upstream + dot(grad_b, centre, turned) + back
    pre_a = pre_ref[...]
    sig_a = jax.nn.sigmoid(pre_a)
    grad_a = (back * mult_a * sig_a * (1.0 + pre_a * (1.0 - sig_a))).astype(bf16)
    grad_keep[...] = jnp.where(c == 0, grad_a[:, :lane], grad_a[:, lane:])
    grad_send[...] = jnp.where(c == 0, grad_a[:, lane:], grad_a[:, :lane])


def term_kernel(
    layout, scale, field_ref, keep_ref, near_ref, own_ref, far0_ref, far1_ref, far2_ref, total
):
    x, y, c, z = place()
    half, width = field_ref.shape[1:]
    keep, near = keep_ref[...], near_ref[...]
    even, odd = jnp.where(c == 0, keep, near), jnp.where(c == 0, near, keep)
    grad = jnp.concatenate([even[:half], odd[:half], even[half:], odd[half:]], axis=0)
    field = jnp.concatenate([field_ref[tile] for tile in range(1, 5)], axis=0)
    over = ((0,), (0,))
    total[:width, :] = dot(field[: 3 * half], grad[half:], over) * scale
    total[width : 2 * width, :] = dot(field, grad, over) * scale
    total[2 * width :, :] = dot(field[half:], grad[: 3 * half], over) * scale
    rows = own_ref.shape[0]
    for (dx, dy), ref in zip(((0, 0), *PLANE_ORDER), (own_ref, far0_ref, far1_ref, far2_ref)):
        start = pl.multiple_of(chosen(layout.start, (x ^ dx, y ^ dy), 0), 8)
        ref[...] = total[pl.ds(start, rows), :].astype(ref.dtype)


def chip_kernel(layout, own_ref, far0_ref, far1_ref, far2_ref, out0, out1, out2, out3, total):
    x, y, c, z = place()
    f32 = jnp.float32
    rows, lane = own_ref.shape
    piece_rows = out0.shape[0]
    value = own_ref[...]
    for ref in (far0_ref, far1_ref, far2_ref):
        value = value + ref[...].astype(f32)
    row = lax.broadcasted_iota(jnp.int32, value.shape, 0)
    edge = jnp.zeros((piece_rows, lane), f32)
    total[0:piece_rows, :] = edge
    held = row < chosen(layout.count, (x, y), 0)
    total[piece_rows : piece_rows + rows, :] = jnp.where(held, value, 0.0)
    total[piece_rows + rows :, :] = edge
    for dz, ref in zip((0, *Z_ORDER), (out0, out1, out2, out3)):
        ends = []
        for core in range(2):
            base = piece_rows + chosen(layout.base, (x, y, z ^ dz, core), -piece_rows)
            ends.append(total[pl.ds(pl.multiple_of(base, 8), piece_rows), :])
        ref[...] = (ends[0] + ends[1]).astype(ref.dtype)


def last_kernel(layout, own_ref, other_ref, out_ref):
    x, y, c, z = place()
    rows = own_ref.shape[0]
    row = lax.broadcasted_iota(jnp.int32, own_ref.shape, 0)
    held = jnp.logical_xor(row < chosen(layout.low, (x, y, z), 0), c == 0)
    own = jnp.where(held, own_ref[...], 0.0)
    other = jnp.where(held, other_ref[...], 0.0)
    out_ref[pl.ds(0, rows, stride=2), :] = jnp.where(c == 0, own, other)
    out_ref[pl.ds(1, rows, stride=2), :] = jnp.where(c == 0, other, own)


def row_shards(inputs, lead_ids, film, flat_weights, cotangent):
    rows, columns, width = inputs.shape[1:]
    half = rows // 2 * columns
    lane = width // 2
    shard_rows = flat_weights.shape[1] // width
    x, y, c, z = place()
    layout = Layout(width, shard_rows)
    bf16, f32 = jnp.bfloat16, jnp.float32
    shape = jax.ShapeDtypeStruct

    def call(name, body, out_shape, scratch, *operands):
        vmem = pl.BlockSpec(memory_space=pltpu.VMEM)
        several = isinstance(out_shape, tuple)
        return pl.pallas_call(
            lambda *refs: body(layout, *refs),
            out_shape=out_shape,
            in_specs=[vmem] * len(operands),
            out_specs=(vmem,) * len(out_shape) if several else vmem,
            scratch_shapes=scratch,
            compiler_params=pltpu.CompilerParams(vmem_limit_bytes=16 * 1024 * 1024),
            name=name,
        )(*operands)

    shard = flat_weights.reshape(2, shard_rows, width)
    left, right = shard[:, :, :lane], shard[:, :, lane:]
    near = moved(jnp.where(c == 0, right, left), dc=1)
    row = lax.broadcasted_iota(jnp.int32, near.shape, 1)
    from_one = row < chosen(layout.low, (x, y, z), 0)
    piece = jnp.where(from_one == (c == 1), jnp.where(c == 0, left, right), near)

    halves_x, halves_ct = (array.reshape(2, half, width) for array in (inputs, cotangent))
    pick = lambda halves, number: lax.dynamic_index_in_dim(halves, number, 0, keepdims=False)
    other = moved(jnp.stack([pick(halves_x, 1 - y), pick(halves_ct, 1 - y)]), dy=1)
    line = [piece, *(moved(piece, dz=dz) for dz in Z_ORDER)]
    *line, halves_x, halves_ct, film = lax.optimization_barrier(
        (*line, halves_x, halves_ct, film)
    )
    mine_x, mine_ct = pick(halves_x, y), pick(halves_ct, y)
    film_row = lax.dynamic_index_in_dim(film, lead_ids[0], 0, keepdims=False)
    near_x0 = moved(mine_x, dc=1)
    line = call(
        "line",
        line_kernel,
        shape((2, layout.column_rows, lane), bf16),
        [pltpu.VMEM((2, layout.column_rows + 2 * shard_rows, lane), f32)],
        *line,
    )
    near_x1 = moved(other[0], dc=1)
    plane = [line, *(moved(line, dx=dx, dy=dy) for dx, dy in PLANE_ORDER)]
    *plane, near_x0, near_x1, mine_x, mine_ct, film_row = lax.optimization_barrier(
        (*plane, near_x0, near_x1, mine_x, mine_ct, film_row)
    )
    own_a, own_b = (jnp.stack([column[k] for column in plane]) for k in range(2))
    near_a, near_b = moved(own_a, dc=1), moved(own_b, dc=1)

    field, pre_a, hidden = call(
        "block_one",
        first_kernel,
        (shape((6, half, width), bf16), shape((2 * half, width), f32), shape((2 * half, width), bf16)),
        [],
        *(mine_x, other, near_x0, near_x1, own_a, near_a, film_row),
    )
    out_keep, out_send, grad_keep, grad_send = call(
        "block_two",
        second_kernel,
        (shape((half, width), bf16),) * 2 + (shape((2 * half, lane), bf16),) * 2,
        [],
        *(pre_a, hidden, mine_ct, other, own_b, near_b, film_row),
    )

    scale = 1.0 / math.sqrt(lax.axis_size(AXES) * rows * columns)
    column = call(
        "terms",
        lambda layout, *refs: term_kernel(layout, scale, *refs),
        (shape((layout.column_rows, lane), f32),) + (shape((layout.column_rows, lane), bf16),) * 3,
        [pltpu.VMEM((3 * width, lane), f32)],
        *(field, grad_keep, moved(grad_send, dc=1)),
    )
    other_out = moved(out_send, dy=1)
    column = [column[0], *(moved(term, dx=dx, dy=dy) for term, (dx, dy) in zip(column[1:], PLANE_ORDER))]
    chip = call(
        "chips",
        chip_kernel,
        (shape((shard_rows, lane), f32),) + (shape((shard_rows, lane), bf16),) * 3,
        [pltpu.VMEM((layout.column_rows + 2 * shard_rows, lane), f32)],
        *column,
    )
    lane_sum = chip[0]
    for term, dz in reversed(list(zip(chip[1:], Z_ORDER))):
        lane_sum = lane_sum + moved(term, dz=dz).astype(f32)

    first = jnp.where(y == 0, out_keep, other_out)
    second = jnp.where(y == 0, other_out, out_keep)
    outputs = jnp.stack([first, second]).reshape(inputs.shape)

    total = call(
        "total",
        last_kernel,
        shape((2 * shard_rows, lane), f32),
        [],
        *(lane_sum, moved(lane_sum, dc=1)),
    )
    return (outputs, total.reshape(-1))


def solution(mesh):
    def whole(inputs, lead_ids, film, flat_weights, cotangent):
        size = mesh.shape
        rows, columns = inputs.shape[1] // size["gy"], inputs.shape[2] // size["gx"]
        plan = row_shards if fits(mesh, rows, columns) else general_shards
        return jax.shard_map(
            plan,
            mesh=mesh,
            in_specs=(
                P("lead", "gy", "gx", None),
                P("lead"),
                P(),
                P(None, AXES),
                P("lead", "gy", "gx", None),
            ),
            out_specs=(P("lead", "gy", "gx", None), P(AXES)),
            check_vma=False,
        )(inputs, lead_ids, film, flat_weights, cotangent)

    return whole
```

```python
import math

import jax
import jax.numpy as jnp
from jax import lax
from jax.experimental import pallas as pl
from jax.experimental.pallas import tpu as pltpu
from jax.sharding import PartitionSpec as P

FIRST_DILATION = 64
SECOND_DILATION = 128
AXES = ("lead", "gy", "gx")


def passed_along(value, axis, steps):
    count = lax.axis_size(axis)
    leading, last = (max(0, -steps), min(count, count - steps))
    return lax.ppermute(value, axis, [(source, source + steps) for source in range(leading, last)])


def shortened(array):
    return jax.tree.map(lambda a: a.astype(jnp.bfloat16) if a.dtype == jnp.float32 else a, array)


def adjacent_cells(weather_field, row_step, col_step):
    row_list = [-1, 0, 1]
    col_list = [-1, 0, 1] if col_step < lax.axis_size("gx") else [0]
    taps = []
    stacked = jnp.stack(
        [
            (
                weather_field
                if row_off == 0
                else passed_along(weather_field, "gy", -row_off * row_step)
            )
            for row_off in row_list
        ]
    )
    columns = [
        (
            stacked
            if col_off == 0
            else passed_along(shortened(stacked), "gx", -col_off * col_step).astype(stacked.dtype)
        )
        for col_off in col_list
    ]
    for col_off in col_list:
        for row_off in row_list:
            taps.append(
                (row_off, col_off, columns[col_list.index(col_off)][row_list.index(row_off)])
            )
    return taps


def lower(taps, weight_four, flipped):
    patch_width = weight_four.shape[-1]
    cols = jnp.concatenate(
        [piece.reshape(-1, patch_width) for row_off, col_off, piece in taps], axis=1
    )
    blocks = []
    for row_off, col_off, piece in taps:
        if flipped:
            blocks.append(weight_four[1 - row_off, 1 - col_off].T)
        else:
            blocks.append(weight_four[row_off + 1, col_off + 1])
    return (cols, jnp.concatenate(blocks, axis=0))


def general_shards(inputs, lead_ids, film, flat_weights, cotangent):
    tile_row_count, tile_column_count, patch_width = (
        inputs.shape[1],
        inputs.shape[2],
        inputs.shape[3],
    )
    gathered = lax.all_gather(flat_weights, AXES, axis=1, tiled=True)
    weight_a = gathered[0].reshape(3, 3, patch_width, patch_width)
    weight_b = gathered[1].reshape(3, 3, patch_width, patch_width)
    film_row = lax.dynamic_index_in_dim(film, lead_ids[0], 0, keepdims=False)
    mult_a = 1.0 + film_row[0]
    shift_a = film_row[1]
    mult_b = 1.0 + film_row[2]
    shift_b = film_row[3]
    weather_field = inputs[0]
    input_kernel_taps = adjacent_cells(
        weather_field, FIRST_DILATION // tile_row_count, FIRST_DILATION // tile_column_count
    )
    input_columns, matrix_a = lower(input_kernel_taps, weight_a, False)
    pre_a = jnp.dot(input_columns, matrix_a, preferred_element_type=jnp.float32) * mult_a + shift_a
    sig_a = jax.nn.sigmoid(pre_a)
    hidden_state = (
        weather_field.reshape(-1, patch_width).astype(jnp.float32) + pre_a * sig_a
    ).astype(jnp.bfloat16)
    taps_hidden = adjacent_cells(
        hidden_state.reshape(tile_row_count, tile_column_count, patch_width),
        SECOND_DILATION // tile_row_count,
        SECOND_DILATION // tile_column_count,
    )
    hidden_columns, matrix_b = lower(taps_hidden, weight_b, False)
    pre_b = jnp.dot(hidden_columns, matrix_b, preferred_element_type=jnp.float32) * mult_b + shift_b
    sig_b = jax.nn.sigmoid(pre_b)
    outputs = (hidden_state.astype(jnp.float32) + pre_b * sig_b).astype(jnp.bfloat16)
    upstream = cotangent[0].reshape(-1, patch_width).astype(jnp.float32)
    second_gradient = (upstream * mult_b * sig_b * (1.0 + pre_b * (1.0 - sig_b))).astype(
        jnp.bfloat16
    )
    taps_grad = adjacent_cells(
        second_gradient.reshape(tile_row_count, tile_column_count, patch_width),
        SECOND_DILATION // tile_row_count,
        SECOND_DILATION // tile_column_count,
    )
    column_gradient, matrix_t = lower(taps_grad, weight_b, True)
    back = upstream + jnp.dot(column_gradient, matrix_t, preferred_element_type=jnp.float32)
    grad_a = (back * mult_a * sig_a * (1.0 + pre_a * (1.0 - sig_a))).astype(jnp.bfloat16)
    scale = 1.0 / math.sqrt(lax.axis_size(AXES) * tile_row_count * tile_column_count)
    products = (
        lax.dot_general(
            input_columns, grad_a, (((0,), (0,)), ((), ())), preferred_element_type=jnp.float32
        )
        * scale
    )
    term = jnp.zeros((3, 3, patch_width, patch_width), jnp.float32)
    for number, (row_off, col_off, piece) in enumerate(input_kernel_taps):
        term = term.at[row_off + 1, col_off + 1].set(
            products[number * patch_width : (number + 1) * patch_width]
        )
    flat_term = term.reshape(lax.axis_size(("lead", "gy")), lax.axis_size("gx"), -1)
    partial_sum = lax.psum_scatter(flat_term, "gx", scatter_dimension=1, tiled=True)
    total = lax.psum_scatter(partial_sum, ("lead", "gy"), scatter_dimension=0, tiled=True)
    return (outputs.reshape(inputs.shape), total.reshape(-1))


def fits(mesh, rows, columns):
    size = mesh.shape
    return (
        tuple(mesh.axis_names) == AXES
        and (size["lead"], size["gy"], size["gx"]) == (2, 4, 4)
        and FIRST_DILATION == rows
        and SECOND_DILATION == 2 * rows
        and FIRST_DILATION // columns >= size["gx"]
    )


def pairs(move):
    number = lambda x, y, c, z: x * 16 + (2 * y + c) * 4 + z
    return [
        (number(x, y, c, z), number(*move(x, y, c, z)))
        for x in range(2)
        for y in range(2)
        for c in range(2)
        for z in range(4)
    ]


def moved(value, dx=0, dy=0, dc=0, dz=0):
    return lax.ppermute(
        value, AXES, pairs(lambda x, y, c, z: (x ^ dx, y ^ dy, c ^ dc, z ^ dz))
    )


Z_ORDER = (3, 2, 1)
PLANE_ORDER = ((1, 1), (1, 0), (0, 1))


def place():
    x, gy, z = (lax.axis_index(axis) for axis in AXES)
    return x, gy // 2, gy % 2, z


def used_rows(width, shard_rows):
    found = []
    for block in range(3):
        start = (3 * block + 1) * width
        row = start
        while row < start + width:
            shard = row // shard_rows
            stop = min((shard + 1) * shard_rows, start + width)
            place = (shard // 16, shard // 8 % 2, shard // 4 % 2, shard % 4)
            found.append((*place, row - shard * shard_rows, stop - row, block * width + row - start))
            row = stop
    return found


def chosen(table, here, otherwise):
    value = otherwise
    for key, entry in table.items():
        if entry != otherwise:
            match = here[0] == key[0]
            for mine, wanted in zip(here[1:], key[1:]):
                match = match & (mine == wanted)
            value = jnp.where(match, entry, value)
    return value


class Layout:
    def __init__(self, width, shard_rows):
        self.pieces = used_rows(width, shard_rows)
        self.start, self.count, self.base, self.first, self.stop = {}, {}, {}, {}, {}
        for cx, cy, cc, cz, first, count, row in self.pieces:
            self.start[cx, cy] = min(self.start.get((cx, cy), 3 * width), row)
            self.count[cx, cy] = self.count.get((cx, cy), 0) + count
        for cx, cy, cc, cz, first, count, row in self.pieces:
            self.base[cx, cy, cz, cc] = row - self.start[cx, cy] - first
            self.first[cx, cy, cz, cc] = first
            self.stop[cx, cy, cz, cc] = first + count
        self.low = {
            key[:3]: stop for key, stop in self.stop.items() if key[3] == 1
        }
        for key, first in self.first.items():
            assert key[3] == 1 or self.low.get(key[:3], 0) <= first
        self.column_rows = max(self.count.values())
        assert all(start + self.column_rows <= 3 * width for start in self.start.values())
        assert len(self.base) == len(self.pieces)


def copy_kernel(layout, value_ref, out_ref):
    out_ref[...] = value_ref[...]


def line_kernel(layout, own_ref, far0_ref, far1_ref, far2_ref, out_ref, total):
    x, y, c, z = place()
    rows = own_ref.shape[1]
    total[...] = jnp.zeros_like(total)
    row = lax.broadcasted_iota(jnp.int32, own_ref.shape[1:], 0)
    for dz, ref in zip((0, *Z_ORDER), (own_ref, far0_ref, far1_ref, far2_ref)):
        for core in range(2):
            here = (x, y, z ^ dz, core)
            first, stop = chosen(layout.first, here, 0), chosen(layout.stop, here, 0)
            base = pl.multiple_of(rows + chosen(layout.base, here, -rows), 8)
            used = (row >= first) & (row < stop)
            for k in range(2):
                value = jnp.where(used, ref[k].astype(jnp.float32), 0.0)
                total[k, pl.ds(base, rows), :] += value
    out_ref[...] = total[:, rows : rows + out_ref.shape[1], :].astype(out_ref.dtype)


def slot(dx, dy):
    found = 0
    for number, (to_x, to_y) in enumerate(PLANE_ORDER):
        found = jnp.where((dx == to_x) & (dy == to_y), number + 1, found)
    return found


def matrix(layout, own_ref, near_ref):
    x, y, c, z = place()
    halves = []
    for ref in (own_ref, near_ref):
        parts = [
            ref[slot(cx ^ x, cy ^ y)][: layout.count[cx, cy]]
            for cx, cy in sorted(layout.start, key=layout.start.get)
        ]
        halves.append(jnp.concatenate(parts, axis=0))
    own, near = halves
    return jnp.concatenate([jnp.where(c == 0, own, near), jnp.where(c == 0, near, own)], axis=1)


def dot(a, b, dims=((1,), (0,))):
    return lax.dot_general(a, b, (dims, ((), ())), preferred_element_type=jnp.float32)


def first_kernel(
    layout, mine_ref, other_ref, near0_ref, near1_ref, own_w, near_w, film_ref,
    field_ref, pre_ref, hidden_ref,
):
    x, y, c, z = place()
    half, width = mine_ref.shape
    near0, near1 = near0_ref[...], near1_ref[...]
    mine, other = mine_ref[...], other_ref[0]
    lo, hi = jnp.where(y == 0, mine, other), jnp.where(y == 0, other, mine)
    near_lo, near_hi = jnp.where(y == 0, near0, near1), jnp.where(y == 0, near1, near0)
    field_ref[0] = jnp.zeros_like(lo)
    field_ref[1] = jnp.where(c == 0, lo, near_lo)
    field_ref[2] = jnp.where(c == 0, near_lo, lo)
    field_ref[3] = jnp.where(c == 0, hi, near_hi)
    field_ref[4] = jnp.where(c == 0, near_hi, hi)
    field_ref[5] = jnp.zeros_like(lo)
    above = jnp.concatenate([field_ref[c], field_ref[c + 2]], axis=0)
    mid = jnp.concatenate([lo, hi], axis=0)
    below = jnp.concatenate([field_ref[c + 2], field_ref[c + 4]], axis=0)
    weight = matrix(layout, own_w, near_w)
    conv = dot(above, weight[:width]) + dot(mid, weight[width : 2 * width])
    conv = conv + dot(below, weight[2 * width :])
    pre = conv * (1.0 + film_ref[0:1, :]) + film_ref[1:2, :]
    pre_ref[...] = pre
    hidden_ref[...] = (mid.astype(jnp.float32) + pre * jax.nn.sigmoid(pre)).astype(hidden_ref.dtype)


def second_kernel(
    layout, pre_ref, hidden_ref, mine_ct, other_ref, own_w, near_w, film_ref,
    out_keep, out_send, grad_keep, grad_send,
):
    x, y, c, z = place()
    half, width = mine_ct.shape
    f32, bf16 = jnp.float32, jnp.bfloat16
    lane = width // 2
    mult_a = 1.0 + film_ref[0:1, :]
    mult_b = 1.0 + film_ref[2:3, :]
    weight = matrix(layout, own_w, near_w)
    up, centre, down = weight[:width], weight[width : 2 * width], weight[2 * width :]
    hidden = hidden_ref[...]
    across = jnp.concatenate([dot(hidden[half:], down), dot(hidden[:half], up)], axis=0)
    pre_b = (dot(hidden, centre) + across) * mult_b + film_ref[3:4, :]
    sig_b = jax.nn.sigmoid(pre_b)
    result = (hidden.astype(f32) + pre_b * sig_b).astype(bf16)
    out_keep[...] = jnp.where(y == 0, result[:half], result[half:])
    out_send[...] = jnp.where(y == 0, result[half:], result[:half])
    mine, other = mine_ct[...], other_ref[1]
    lo, hi = jnp.where(y == 0, mine, other), jnp.where(y == 0, other, mine)
    upstream = jnp.concatenate([lo, hi], axis=0).astype(f32)
    grad_b = (upstream * mult_b * sig_b * (1.0 + pre_b * (1.0 - sig_b))).astype(bf16)
    turned = ((1,), (1,))
    back = jnp.concatenate(
        [dot(grad_b[half:], up, turned), dot(grad_b[:half], down, turned)], axis=0
    )
    back = upstream + dot(grad_b, centre, turned) + back
    pre_a = pre_ref[...]
    sig_a = jax.nn.sigmoid(pre_a)
    grad_a = (back * mult_a * sig_a * (1.0 + pre_a * (1.0 - sig_a))).astype(bf16)
    grad_keep[...] = jnp.where(c == 0, grad_a[:, :lane], grad_a[:, lane:])
    grad_send[...] = jnp.where(c == 0, grad_a[:, lane:], grad_a[:, :lane])


def term_kernel(
    layout, scale, field_ref, keep_ref, near_ref, own_ref, far0_ref, far1_ref, far2_ref, total
):
    x, y, c, z = place()
    half, width = field_ref.shape[1:]
    keep, near = keep_ref[...], near_ref[...]
    even, odd = jnp.where(c == 0, keep, near), jnp.where(c == 0, near, keep)
    grad = jnp.concatenate([even[:half], odd[:half], even[half:], odd[half:]], axis=0)
    field = jnp.concatenate([field_ref[tile] for tile in range(1, 5)], axis=0)
    over = ((0,), (0,))
    total[:width, :] = dot(field[: 3 * half], grad[half:], over) * scale
    total[width : 2 * width, :] = dot(field, grad, over) * scale
    total[2 * width :, :] = dot(field[half:], grad[: 3 * half], over) * scale
    rows = own_ref.shape[0]
    for (dx, dy), ref in zip(((0, 0), *PLANE_ORDER), (own_ref, far0_ref, far1_ref, far2_ref)):
        start = pl.multiple_of(chosen(layout.start, (x ^ dx, y ^ dy), 0), 8)
        ref[...] = total[pl.ds(start, rows), :].astype(ref.dtype)


def chip_kernel(layout, own_ref, far0_ref, far1_ref, far2_ref, out0, out1, out2, out3, total):
    x, y, c, z = place()
    f32 = jnp.float32
    rows, lane = own_ref.shape
    piece_rows = out0.shape[0]
    value = own_ref[...]
    for ref in (far0_ref, far1_ref, far2_ref):
        value = value + ref[...].astype(f32)
    row = lax.broadcasted_iota(jnp.int32, value.shape, 0)
    edge = jnp.zeros((piece_rows, lane), f32)
    total[0:piece_rows, :] = edge
    held = row < chosen(layout.count, (x, y), 0)
    total[piece_rows : piece_rows + rows, :] = jnp.where(held, value, 0.0)
    total[piece_rows + rows :, :] = edge
    for dz, ref in zip((0, *Z_ORDER), (out0, out1, out2, out3)):
        ends = []
        for core in range(2):
            base = piece_rows + chosen(layout.base, (x, y, z ^ dz, core), -piece_rows)
            ends.append(total[pl.ds(pl.multiple_of(base, 8), piece_rows), :])
        ref[...] = (ends[0] + ends[1]).astype(ref.dtype)


def last_kernel(layout, own_ref, other_ref, out_ref):
    x, y, c, z = place()
    rows = own_ref.shape[0]
    row = lax.broadcasted_iota(jnp.int32, own_ref.shape, 0)
    held = jnp.logical_xor(row < chosen(layout.low, (x, y, z), 0), c == 0)
    own = jnp.where(held, own_ref[...], 0.0)
    other = jnp.where(held, other_ref[...], 0.0)
    out_ref[pl.ds(0, rows, stride=2), :] = jnp.where(c == 0, own, other)
    out_ref[pl.ds(1, rows, stride=2), :] = jnp.where(c == 0, other, own)


def row_shards(inputs, lead_ids, film, flat_weights, cotangent):
    rows, columns, width = inputs.shape[1:]
    half = rows // 2 * columns
    lane = width // 2
    shard_rows = flat_weights.shape[1] // width
    x, y, c, z = place()
    layout = Layout(width, shard_rows)
    bf16, f32 = jnp.bfloat16, jnp.float32
    shape = jax.ShapeDtypeStruct

    def call(name, body, out_shape, scratch, *operands, cost=0):
        vmem = pl.BlockSpec(memory_space=pltpu.VMEM)
        several = isinstance(out_shape, tuple)
        return pl.pallas_call(
            lambda *refs: body(layout, *refs),
            out_shape=out_shape,
            in_specs=[vmem] * len(operands),
            out_specs=(vmem,) * len(out_shape) if several else vmem,
            scratch_shapes=scratch,
            compiler_params=pltpu.CompilerParams(vmem_limit_bytes=16 * 1024 * 1024),
            cost_estimate=pl.CostEstimate(flops=cost * 10**9, bytes_accessed=0, transcendentals=0) if cost else None,
            name=name,
        )(*operands)

    near_flat = moved(flat_weights, dc=1)
    halves_x, halves_ct = (array.reshape(2, half, width) for array in (inputs, cotangent))
    pick = lambda halves, number: lax.dynamic_index_in_dim(halves, number, 0, keepdims=False)
    give = jnp.stack([pick(halves_x, 1 - y), pick(halves_ct, 1 - y)])
    near_flat, give = lax.optimization_barrier((near_flat, give))
    shard = moved(near_flat, dc=1).reshape(2, shard_rows, width)
    give = call("give", copy_kernel, shape(give.shape, bf16), [], give, cost=3)
    other = moved(give, dy=1)
    left, right = shard[:, :, :lane], shard[:, :, lane:]
    near = near_flat.reshape(shard.shape)
    near = jnp.where(c == 0, near[:, :, :lane], near[:, :, lane:])
    row = lax.broadcasted_iota(jnp.int32, near.shape, 1)
    from_one = row < chosen(layout.low, (x, y, z), 0)
    piece = jnp.where(from_one == (c == 1), jnp.where(c == 0, left, right), near)

    halves_x, halves_ct = (array.reshape(2, half, width) for array in (inputs, cotangent))
    pick = lambda halves, number: lax.dynamic_index_in_dim(halves, number, 0, keepdims=False)
    line = [piece, *(moved(piece, dz=dz) for dz in Z_ORDER)]
    *line, halves_x, halves_ct, film = lax.optimization_barrier(
        (*line, halves_x, halves_ct, film)
    )
    mine_x, mine_ct = pick(halves_x, y), pick(halves_ct, y)
    film_row = lax.dynamic_index_in_dim(film, lead_ids[0], 0, keepdims=False)
    near_x0 = moved(mine_x, dc=1)
    line = call(
        "line",
        line_kernel,
        shape((2, layout.column_rows, lane), bf16),
        [pltpu.VMEM((2, layout.column_rows + 2 * shard_rows, lane), f32)],
        *line,
    )
    near_x1 = moved(other[0], dc=1)
    plane = [line, *(moved(line, dx=dx, dy=dy) for dx, dy in PLANE_ORDER)]
    *plane, near_x0, near_x1, mine_x, mine_ct, film_row = lax.optimization_barrier(
        (*plane, near_x0, near_x1, mine_x, mine_ct, film_row)
    )
    own_a, own_b = (jnp.stack([column[k] for column in plane]) for k in range(2))
    near_a, near_b = moved(own_a, dc=1), moved(own_b, dc=1)

    field, pre_a, hidden = call(
        "block_one",
        first_kernel,
        (shape((6, half, width), bf16), shape((2 * half, width), f32), shape((2 * half, width), bf16)),
        [],
        *(mine_x, other, near_x0, near_x1, own_a, near_a, film_row),
    )
    out_keep, out_send, grad_keep, grad_send = call(
        "block_two",
        second_kernel,
        (shape((half, width), bf16),) * 2 + (shape((2 * half, lane), bf16),) * 2,
        [],
        *(pre_a, hidden, mine_ct, other, own_b, near_b, film_row),
    )

    scale = 1.0 / math.sqrt(lax.axis_size(AXES) * rows * columns)
    column = call(
        "terms",
        lambda layout, *refs: term_kernel(layout, scale, *refs),
        (shape((layout.column_rows, lane), f32),) + (shape((layout.column_rows, lane), bf16),) * 3,
        [pltpu.VMEM((3 * width, lane), f32)],
        *(field, grad_keep, moved(grad_send, dc=1)),
    )
    other_out = moved(out_send, dy=1)
    column = [column[0], *(moved(term, dx=dx, dy=dy) for term, (dx, dy) in zip(column[1:], PLANE_ORDER))]
    chip = call(
        "chips",
        chip_kernel,
        (shape((shard_rows, lane), f32),) + (shape((shard_rows, lane), bf16),) * 3,
        [pltpu.VMEM((layout.column_rows + 2 * shard_rows, lane), f32)],
        *column,
    )
    lane_sum = chip[0]
    for term, dz in reversed(list(zip(chip[1:], Z_ORDER))):
        lane_sum = lane_sum + moved(term, dz=dz).astype(f32)

    first = jnp.where(y == 0, out_keep, other_out)
    second = jnp.where(y == 0, other_out, out_keep)
    outputs = jnp.stack([first, second]).reshape(inputs.shape)

    total = call(
        "total",
        last_kernel,
        shape((2 * shard_rows, lane), f32),
        [],
        *(lane_sum, moved(lane_sum, dc=1)),
    )
    return (outputs, total.reshape(-1))


def solution(mesh):
    def whole(inputs, lead_ids, film, flat_weights, cotangent):
        size = mesh.shape
        rows, columns = inputs.shape[1] // size["gy"], inputs.shape[2] // size["gx"]
        plan = row_shards if fits(mesh, rows, columns) else general_shards
        return jax.shard_map(
            plan,
            mesh=mesh,
            in_specs=(
                P("lead", "gy", "gx", None),
                P("lead"),
                P(),
                P(None, AXES),
                P("lead", "gy", "gx", None),
            ),
            out_specs=(P("lead", "gy", "gx", None), P(AXES)),
            check_vma=False,
        )(inputs, lead_ids, film, flat_weights, cotangent)

    return whole
```

```python
import math

import jax
import jax.numpy as jnp
from jax import lax
from jax.experimental import pallas as pl
from jax.experimental.pallas import tpu as pltpu
from jax.sharding import PartitionSpec as P

FIRST_DILATION = 64
SECOND_DILATION = 128
AXES = ("lead", "gy", "gx")


def passed_along(value, axis, steps):
    count = lax.axis_size(axis)
    leading, last = (max(0, -steps), min(count, count - steps))
    return lax.ppermute(value, axis, [(source, source + steps) for source in range(leading, last)])


def shortened(array):
    return jax.tree.map(lambda a: a.astype(jnp.bfloat16) if a.dtype == jnp.float32 else a, array)


def adjacent_cells(weather_field, row_step, col_step):
    row_list = [-1, 0, 1]
    col_list = [-1, 0, 1] if col_step < lax.axis_size("gx") else [0]
    taps = []
    stacked = jnp.stack(
        [
            (
                weather_field
                if row_off == 0
                else passed_along(weather_field, "gy", -row_off * row_step)
            )
            for row_off in row_list
        ]
    )
    columns = [
        (
            stacked
            if col_off == 0
            else passed_along(shortened(stacked), "gx", -col_off * col_step).astype(stacked.dtype)
        )
        for col_off in col_list
    ]
    for col_off in col_list:
        for row_off in row_list:
            taps.append(
                (row_off, col_off, columns[col_list.index(col_off)][row_list.index(row_off)])
            )
    return taps


def lower(taps, weight_four, flipped):
    patch_width = weight_four.shape[-1]
    cols = jnp.concatenate(
        [piece.reshape(-1, patch_width) for row_off, col_off, piece in taps], axis=1
    )
    blocks = []
    for row_off, col_off, piece in taps:
        if flipped:
            blocks.append(weight_four[1 - row_off, 1 - col_off].T)
        else:
            blocks.append(weight_four[row_off + 1, col_off + 1])
    return (cols, jnp.concatenate(blocks, axis=0))


def general_shards(inputs, lead_ids, film, flat_weights, cotangent):
    tile_row_count, tile_column_count, patch_width = (
        inputs.shape[1],
        inputs.shape[2],
        inputs.shape[3],
    )
    gathered = lax.all_gather(flat_weights, AXES, axis=1, tiled=True)
    weight_a = gathered[0].reshape(3, 3, patch_width, patch_width)
    weight_b = gathered[1].reshape(3, 3, patch_width, patch_width)
    film_row = lax.dynamic_index_in_dim(film, lead_ids[0], 0, keepdims=False)
    mult_a = 1.0 + film_row[0]
    shift_a = film_row[1]
    mult_b = 1.0 + film_row[2]
    shift_b = film_row[3]
    weather_field = inputs[0]
    input_kernel_taps = adjacent_cells(
        weather_field, FIRST_DILATION // tile_row_count, FIRST_DILATION // tile_column_count
    )
    input_columns, matrix_a = lower(input_kernel_taps, weight_a, False)
    pre_a = jnp.dot(input_columns, matrix_a, preferred_element_type=jnp.float32) * mult_a + shift_a
    sig_a = jax.nn.sigmoid(pre_a)
    hidden_state = (
        weather_field.reshape(-1, patch_width).astype(jnp.float32) + pre_a * sig_a
    ).astype(jnp.bfloat16)
    taps_hidden = adjacent_cells(
        hidden_state.reshape(tile_row_count, tile_column_count, patch_width),
        SECOND_DILATION // tile_row_count,
        SECOND_DILATION // tile_column_count,
    )
    hidden_columns, matrix_b = lower(taps_hidden, weight_b, False)
    pre_b = jnp.dot(hidden_columns, matrix_b, preferred_element_type=jnp.float32) * mult_b + shift_b
    sig_b = jax.nn.sigmoid(pre_b)
    outputs = (hidden_state.astype(jnp.float32) + pre_b * sig_b).astype(jnp.bfloat16)
    upstream = cotangent[0].reshape(-1, patch_width).astype(jnp.float32)
    second_gradient = (upstream * mult_b * sig_b * (1.0 + pre_b * (1.0 - sig_b))).astype(
        jnp.bfloat16
    )
    taps_grad = adjacent_cells(
        second_gradient.reshape(tile_row_count, tile_column_count, patch_width),
        SECOND_DILATION // tile_row_count,
        SECOND_DILATION // tile_column_count,
    )
    column_gradient, matrix_t = lower(taps_grad, weight_b, True)
    back = upstream + jnp.dot(column_gradient, matrix_t, preferred_element_type=jnp.float32)
    grad_a = (back * mult_a * sig_a * (1.0 + pre_a * (1.0 - sig_a))).astype(jnp.bfloat16)
    scale = 1.0 / math.sqrt(lax.axis_size(AXES) * tile_row_count * tile_column_count)
    products = (
        lax.dot_general(
            input_columns, grad_a, (((0,), (0,)), ((), ())), preferred_element_type=jnp.float32
        )
        * scale
    )
    term = jnp.zeros((3, 3, patch_width, patch_width), jnp.float32)
    for number, (row_off, col_off, piece) in enumerate(input_kernel_taps):
        term = term.at[row_off + 1, col_off + 1].set(
            products[number * patch_width : (number + 1) * patch_width]
        )
    flat_term = term.reshape(lax.axis_size(("lead", "gy")), lax.axis_size("gx"), -1)
    partial_sum = lax.psum_scatter(flat_term, "gx", scatter_dimension=1, tiled=True)
    total = lax.psum_scatter(partial_sum, ("lead", "gy"), scatter_dimension=0, tiled=True)
    return (outputs.reshape(inputs.shape), total.reshape(-1))


def fits(mesh, rows, columns):
    size = mesh.shape
    return (
        tuple(mesh.axis_names) == AXES
        and (size["lead"], size["gy"], size["gx"]) == (2, 4, 4)
        and FIRST_DILATION == rows
        and SECOND_DILATION == 2 * rows
        and FIRST_DILATION // columns >= size["gx"]
    )


def pairs(move):
    number = lambda x, y, c, z: x * 16 + (2 * y + c) * 4 + z
    return [
        (number(x, y, c, z), number(*move(x, y, c, z)))
        for x in range(2)
        for y in range(2)
        for c in range(2)
        for z in range(4)
    ]


def moved(value, dx=0, dy=0, dc=0, dz=0):
    return lax.ppermute(
        value, AXES, pairs(lambda x, y, c, z: (x ^ dx, y ^ dy, c ^ dc, z ^ dz))
    )


FIRST_ROUND = ((1, 2), (0, 2), (1, 0))
SECOND_ROUND = ((1, 1), (0, 1), (1, 0))


def place():
    x, gy, z = (lax.axis_index(axis) for axis in AXES)
    return x, gy // 2, gy % 2, z


def used_rows(width, shard_rows):
    found = []
    for block in range(3):
        start = (3 * block + 1) * width
        row = start
        while row < start + width:
            shard = row // shard_rows
            stop = min((shard + 1) * shard_rows, start + width)
            place = (shard // 16, shard // 8 % 2, shard // 4 % 2, shard % 4)
            found.append((*place, row - shard * shard_rows, stop - row, block * width + row - start))
            row = stop
    return found


def chosen(table, here, otherwise):
    value = otherwise
    for key, entry in table.items():
        if entry != otherwise:
            match = here[0] == key[0]
            for mine, wanted in zip(here[1:], key[1:]):
                match = match & (mine == wanted)
            value = jnp.where(match, entry, value)
    return value


class Layout:
    def __init__(self, width, shard_rows):
        self.pieces = {(x, part): [] for x in range(2) for part in range(2)}
        self.base, self.first, self.stop = {}, {}, {}
        held = dict.fromkeys(self.pieces, 0)
        for cx, cy, cc, cz, first, count, row in used_rows(width, shard_rows):
            group, key = (cx, cz % 2), (cx, cy, cz, cc)
            assert key not in self.base
            self.pieces[group].append((held[group], count, row))
            self.base[key] = held[group] - first
            self.first[key], self.stop[key] = first, first + count
            held[group] += count
        self.rows = max(held.values())
        self.low = {key[:3]: stop for key, stop in self.stop.items() if key[3] == 1}
        for key, first in self.first.items():
            assert key[3] == 1 or self.low.get(key[:3], 0) <= first


def copy_kernel(layout, value_ref, out_ref):
    out_ref[...] = value_ref[...]


def group_kernel(layout, own_ref, far0_ref, far1_ref, far2_ref, out_ref, total):
    x, y, c, z = place()
    rows = own_ref.shape[1]
    total[...] = jnp.zeros_like(total)
    row = lax.broadcasted_iota(jnp.int32, own_ref.shape[1:], 0)
    for (dy, dz), ref in zip(((0, 0), *FIRST_ROUND), (own_ref, far0_ref, far1_ref, far2_ref)):
        for core in range(2):
            here = (x, y ^ dy, z ^ dz, core)
            first, stop = chosen(layout.first, here, 0), chosen(layout.stop, here, 0)
            base = pl.multiple_of(rows + chosen(layout.base, here, -rows), 8)
            used = (row >= first) & (row < stop)
            for k in range(2):
                value = jnp.where(used, ref[k].astype(jnp.float32), 0.0)
                total[k, pl.ds(base, rows), :] += value
    out_ref[...] = total[:, rows : rows + out_ref.shape[1], :].astype(out_ref.dtype)


def slot(dx, dz):
    found = 0
    for number, (to_x, to_z) in enumerate(SECOND_ROUND):
        found = jnp.where((dx == to_x) & (dz == to_z), number + 1, found)
    return found


def order_kernel(layout, own_ref, far0_ref, far1_ref, far2_ref, a_ref, b_ref, held, total):
    x, y, c, z = place()
    for number, ref in enumerate((own_ref, far0_ref, far1_ref, far2_ref)):
        held[number] = ref[...].astype(jnp.float32)
    for (cx, part), pieces in layout.pieces.items():
        number = slot(cx ^ x, part ^ (z % 2))
        for start, count, row in pieces:
            total[:, row : row + count, :] = held[number, :, start : start + count, :]
    a_ref[...] = total[0].astype(a_ref.dtype)
    b_ref[...] = total[1].astype(b_ref.dtype)


def matrix(own_ref, near_ref):
    c = place()[2]
    own, near = own_ref[...], near_ref[...]
    return jnp.concatenate([jnp.where(c == 0, own, near), jnp.where(c == 0, near, own)], axis=1)


def dot(a, b, dims=((1,), (0,))):
    return lax.dot_general(a, b, (dims, ((), ())), preferred_element_type=jnp.float32)


def first_kernel(
    layout, mine_ref, other_ref, near0_ref, near1_ref, own_w, near_w, film_ref,
    field_ref, slope_ref, hidden_ref,
):
    x, y, c, z = place()
    half, width = mine_ref.shape
    near0, near1 = near0_ref[...], near1_ref[...]
    mine, other = mine_ref[...], other_ref[0]
    lo, hi = jnp.where(y == 0, mine, other), jnp.where(y == 0, other, mine)
    near_lo, near_hi = jnp.where(y == 0, near0, near1), jnp.where(y == 0, near1, near0)
    field_ref[0] = jnp.zeros_like(lo)
    field_ref[1] = jnp.where(c == 0, lo, near_lo)
    field_ref[2] = jnp.where(c == 0, near_lo, lo)
    field_ref[3] = jnp.where(c == 0, hi, near_hi)
    field_ref[4] = jnp.where(c == 0, near_hi, hi)
    field_ref[5] = jnp.zeros_like(lo)
    above = jnp.concatenate([field_ref[c], field_ref[c + 2]], axis=0)
    mid = jnp.concatenate([lo, hi], axis=0)
    below = jnp.concatenate([field_ref[c + 2], field_ref[c + 4]], axis=0)
    weight = matrix(own_w, near_w)
    conv = dot(above, weight[:width]) + dot(mid, weight[width : 2 * width])
    conv = conv + dot(below, weight[2 * width :])
    pre = conv * (1.0 + film_ref[0:1, :]) + film_ref[1:2, :]
    sig = jax.nn.sigmoid(pre)
    lift = pre * sig
    hidden_ref[...] = (mid.astype(jnp.float32) + lift).astype(hidden_ref.dtype)
    slope_ref[...] = (1.0 + film_ref[0:1, :]) * (sig + lift * (1.0 - sig))


def second_kernel(
    layout, slope_ref, hidden_ref, mine_ct, other_ref, own_w, near_w, film_ref,
    out_keep, out_send, grad_keep, grad_send,
):
    x, y, c, z = place()
    half, width = mine_ct.shape
    f32, bf16 = jnp.float32, jnp.bfloat16
    lane = width // 2
    mult_b = 1.0 + film_ref[2:3, :]
    weight = matrix(own_w, near_w)
    up, centre, down = weight[:width], weight[width : 2 * width], weight[2 * width :]
    hidden = hidden_ref[...]
    across = jnp.concatenate([dot(hidden[half:], down), dot(hidden[:half], up)], axis=0)
    pre_b = (dot(hidden, centre) + across) * mult_b + film_ref[3:4, :]
    sig_b = jax.nn.sigmoid(pre_b)
    lift_b = pre_b * sig_b
    result = (hidden.astype(f32) + lift_b).astype(bf16)
    out_keep[...] = jnp.where(y == 0, result[:half], result[half:])
    out_send[...] = jnp.where(y == 0, result[half:], result[:half])
    mine, other = mine_ct[...], other_ref[1]
    lo, hi = jnp.where(y == 0, mine, other), jnp.where(y == 0, other, mine)
    upstream = jnp.concatenate([lo, hi], axis=0).astype(f32)
    grad_b = (upstream * (mult_b * (sig_b + lift_b * (1.0 - sig_b)))).astype(bf16)
    turned = ((1,), (1,))
    back = jnp.concatenate(
        [dot(grad_b[half:], up, turned), dot(grad_b[:half], down, turned)], axis=0
    )
    back = upstream + dot(grad_b, centre, turned) + back
    grad_a = (back * slope_ref[...]).astype(bf16)
    grad_keep[...] = jnp.where(c == 0, grad_a[:, :lane], grad_a[:, lane:])
    grad_send[...] = jnp.where(c == 0, grad_a[:, lane:], grad_a[:, :lane])


def term_kernel(
    layout, scale, field_ref, keep_ref, near_ref, own_ref, far0_ref, far1_ref, far2_ref, total, groups
):
    x, y, c, z = place()
    half, width = field_ref.shape[1:]
    keep, near = keep_ref[...], near_ref[...]
    even, odd = jnp.where(c == 0, keep, near), jnp.where(c == 0, near, keep)
    grad = jnp.concatenate([even[:half], odd[:half], even[half:], odd[half:]], axis=0)
    field = jnp.concatenate([field_ref[tile] for tile in range(1, 5)], axis=0)
    none = jnp.zeros_like(grad[:half])
    below = jnp.concatenate([grad[half:], none], axis=0)
    above = jnp.concatenate([none, grad[: 3 * half]], axis=0)
    sums = dot(field, jnp.concatenate([below, grad, above], axis=1), ((0,), (0,))) * scale
    lane = width // 2
    for number in range(3):
        total[number * width : (number + 1) * width, :] = sums[:, number * lane : (number + 1) * lane]
    for number, pieces in enumerate(layout.pieces.values()):
        for start, count, row in pieces:
            groups[number, start : start + count, :] = total[row : row + count, :]
    for (dx, dz), ref in zip(((0, 0), *SECOND_ROUND), (own_ref, far0_ref, far1_ref, far2_ref)):
        number = 2 * (x ^ dx) + (z ^ dz) % 2
        ref[...] = groups[number].astype(ref.dtype)


def chip_kernel(layout, own_ref, far0_ref, far1_ref, far2_ref, out0, out1, out2, out3, total):
    x, y, c, z = place()
    f32 = jnp.float32
    rows, lane = own_ref.shape
    piece_rows = out0.shape[0]
    value = own_ref[...]
    for ref in (far0_ref, far1_ref, far2_ref):
        value = value + ref[...].astype(f32)
    edge = jnp.zeros((piece_rows, lane), f32)
    total[0:piece_rows, :] = edge
    total[piece_rows : piece_rows + rows, :] = value
    total[piece_rows + rows :, :] = edge
    row = lax.broadcasted_iota(jnp.int32, out0.shape, 0)
    for (dy, dz), ref in zip(((0, 0), *FIRST_ROUND), (out0, out1, out2, out3)):
        piece = edge
        for core in range(2):
            here = (x, y ^ dy, z ^ dz, core)
            base = piece_rows + chosen(layout.base, here, -piece_rows)
            used = (row >= chosen(layout.first, here, 0)) & (row < chosen(layout.stop, here, 0))
            piece = jnp.where(used, total[pl.ds(pl.multiple_of(base, 8), piece_rows), :], piece)
        ref[...] = piece.astype(ref.dtype)


def last_kernel(layout, own_ref, other_ref, out_ref):
    x, y, c, z = place()
    rows = own_ref.shape[0]
    row = lax.broadcasted_iota(jnp.int32, own_ref.shape, 0)
    held = jnp.logical_xor(row < chosen(layout.low, (x, y, z), 0), c == 0)
    own = jnp.where(held, own_ref[...], 0.0)
    other = jnp.where(held, other_ref[...], 0.0)
    out_ref[pl.ds(0, rows, stride=2), :] = jnp.where(c == 0, own, other)
    out_ref[pl.ds(1, rows, stride=2), :] = jnp.where(c == 0, other, own)


def row_shards(inputs, lead_ids, film, flat_weights, cotangent):
    rows, columns, width = inputs.shape[1:]
    half = rows // 2 * columns
    lane = width // 2
    shard_rows = flat_weights.shape[1] // width
    x, y, c, z = place()
    layout = Layout(width, shard_rows)
    bf16, f32 = jnp.bfloat16, jnp.float32
    shape = jax.ShapeDtypeStruct

    def call(name, body, out_shape, scratch, *operands, cost=0):
        vmem = pl.BlockSpec(memory_space=pltpu.VMEM)
        several = isinstance(out_shape, tuple)
        return pl.pallas_call(
            lambda *refs: body(layout, *refs),
            out_shape=out_shape,
            in_specs=[vmem] * len(operands),
            out_specs=(vmem,) * len(out_shape) if several else vmem,
            scratch_shapes=scratch,
            compiler_params=pltpu.CompilerParams(vmem_limit_bytes=16 * 1024 * 1024),
            cost_estimate=pl.CostEstimate(flops=cost * 10**9, bytes_accessed=0, transcendentals=0) if cost else None,
            name=name,
        )(*operands)

    shard = flat_weights.reshape(2, shard_rows, width)
    left, right = shard[:, :, :lane], shard[:, :, lane:]
    near = moved(flat_weights, dc=1).reshape(shard.shape)
    near = jnp.where(c == 0, near[:, :, :lane], near[:, :, lane:])
    row = lax.broadcasted_iota(jnp.int32, near.shape, 1)
    from_one = row < chosen(layout.low, (x, y, z), 0)
    piece = jnp.where(from_one == (c == 1), jnp.where(c == 0, left, right), near)

    halves_x, halves_ct = (array.reshape(2, half, width) for array in (inputs, cotangent))
    pick = lambda halves, number: lax.dynamic_index_in_dim(halves, number, 0, keepdims=False)
    piece, halves_x, halves_ct = lax.optimization_barrier((piece, halves_x, halves_ct))
    give = jnp.stack([pick(halves_x, 1 - y), pick(halves_ct, 1 - y)])
    give = call("give", copy_kernel, shape(give.shape, bf16), [], give, cost=3)
    other = moved(give, dy=1)
    line = [piece, *(moved(piece, dy=dy, dz=dz) for dy, dz in FIRST_ROUND)]
    *line, halves_x, halves_ct, film = lax.optimization_barrier(
        (*line, halves_x, halves_ct, film)
    )
    mine_x, mine_ct = pick(halves_x, y), pick(halves_ct, y)
    film_row = lax.dynamic_index_in_dim(film, lead_ids[0], 0, keepdims=False)
    near_x0 = moved(mine_x, dc=1)
    group = call(
        "group",
        group_kernel,
        shape((2, layout.rows, lane), bf16),
        [pltpu.VMEM((2, layout.rows + 2 * shard_rows, lane), f32)],
        *line,
        cost=6,
    )
    near_x1 = moved(other[0], dc=1)
    groups = [group, *(moved(group, dx=dx, dz=dz) for dx, dz in SECOND_ROUND)]
    *groups, near_x0, near_x1, mine_x, mine_ct, film_row = lax.optimization_barrier(
        (*groups, near_x0, near_x1, mine_x, mine_ct, film_row)
    )
    own_a, own_b = call(
        "order",
        order_kernel,
        (shape((3 * width, lane), bf16),) * 2,
        [pltpu.VMEM((4, 2, layout.rows, lane), f32), pltpu.VMEM((2, 3 * width, lane), f32)],
        *groups,
    )
    near_a, near_b = moved(own_a, dc=1), moved(own_b, dc=1)

    field, slope_a, hidden = call(
        "block_one",
        first_kernel,
        (shape((6, half, width), bf16), shape((2 * half, width), f32), shape((2 * half, width), bf16)),
        [],
        *(mine_x, other, near_x0, near_x1, own_a, near_a, film_row),
    )
    out_keep, out_send, grad_keep, grad_send = call(
        "block_two",
        second_kernel,
        (shape((half, width), bf16),) * 2 + (shape((2 * half, lane), bf16),) * 2,
        [],
        *(slope_a, hidden, mine_ct, other, own_b, near_b, film_row),
    )

    scale = 1.0 / math.sqrt(lax.axis_size(AXES) * rows * columns)
    terms = call(
        "terms",
        lambda layout, *refs: term_kernel(layout, scale, *refs),
        (shape((layout.rows, lane), f32),) + (shape((layout.rows, lane), bf16),) * 3,
        [pltpu.VMEM((3 * width, lane), f32), pltpu.VMEM((4, layout.rows, lane), f32)],
        *(field, grad_keep, moved(grad_send, dc=1)),
    )
    other_out = moved(out_send, dy=1)
    terms = [terms[0], *(moved(term, dx=dx, dz=dz) for term, (dx, dz) in zip(terms[1:], SECOND_ROUND))]
    chip = call(
        "chips",
        chip_kernel,
        (shape((shard_rows, lane), f32),) + (shape((shard_rows, lane), bf16),) * 3,
        [pltpu.VMEM((layout.rows + 2 * shard_rows, lane), f32)],
        *terms,
    )
    lane_sum = chip[0]
    for term, (dy, dz) in zip(chip[1:], FIRST_ROUND):
        lane_sum = lane_sum + moved(term, dy=dy, dz=dz).astype(f32)

    first = jnp.where(y == 0, out_keep, other_out)
    second = jnp.where(y == 0, other_out, out_keep)
    outputs = jnp.stack([first, second]).reshape(inputs.shape)

    total = call(
        "total",
        last_kernel,
        shape((2 * shard_rows, lane), f32),
        [],
        *(lane_sum, moved(lane_sum, dc=1)),
    )
    return (outputs, total.reshape(-1))


def solution(mesh):
    def whole(inputs, lead_ids, film, flat_weights, cotangent):
        size = mesh.shape
        rows, columns = inputs.shape[1] // size["gy"], inputs.shape[2] // size["gx"]
        plan = row_shards if fits(mesh, rows, columns) else general_shards
        return jax.shard_map(
            plan,
            mesh=mesh,
            in_specs=(
                P("lead", "gy", "gx", None),
                P("lead"),
                P(),
                P(None, AXES),
                P("lead", "gy", "gx", None),
            ),
            out_specs=(P("lead", "gy", "gx", None), P(AXES)),
            check_vma=False,
        )(inputs, lead_ids, film, flat_weights, cotangent)

    return whole
```

```python
import math

import jax
import jax.numpy as jnp
from jax import lax
from jax.experimental import pallas as pl
from jax.experimental.pallas import tpu as pltpu
from jax.sharding import PartitionSpec as P

FIRST_DILATION = 64
SECOND_DILATION = 128
AXES = ("lead", "gy", "gx")


def passed_along(value, axis, steps):
    count = lax.axis_size(axis)
    leading, last = (max(0, -steps), min(count, count - steps))
    return lax.ppermute(value, axis, [(source, source + steps) for source in range(leading, last)])


def shortened(array):
    return jax.tree.map(lambda a: a.astype(jnp.bfloat16) if a.dtype == jnp.float32 else a, array)


def adjacent_cells(weather_field, row_step, col_step):
    row_list = [-1, 0, 1]
    col_list = [-1, 0, 1] if col_step < lax.axis_size("gx") else [0]
    taps = []
    stacked = jnp.stack(
        [
            (
                weather_field
                if row_off == 0
                else passed_along(weather_field, "gy", -row_off * row_step)
            )
            for row_off in row_list
        ]
    )
    columns = [
        (
            stacked
            if col_off == 0
            else passed_along(shortened(stacked), "gx", -col_off * col_step).astype(stacked.dtype)
        )
        for col_off in col_list
    ]
    for col_off in col_list:
        for row_off in row_list:
            taps.append(
                (row_off, col_off, columns[col_list.index(col_off)][row_list.index(row_off)])
            )
    return taps


def lower(taps, weight_four, flipped):
    patch_width = weight_four.shape[-1]
    cols = jnp.concatenate(
        [piece.reshape(-1, patch_width) for row_off, col_off, piece in taps], axis=1
    )
    blocks = []
    for row_off, col_off, piece in taps:
        if flipped:
            blocks.append(weight_four[1 - row_off, 1 - col_off].T)
        else:
            blocks.append(weight_four[row_off + 1, col_off + 1])
    return (cols, jnp.concatenate(blocks, axis=0))


def general_shards(inputs, lead_ids, film, flat_weights, cotangent):
    tile_row_count, tile_column_count, patch_width = (
        inputs.shape[1],
        inputs.shape[2],
        inputs.shape[3],
    )
    gathered = lax.all_gather(flat_weights, AXES, axis=1, tiled=True)
    weight_a = gathered[0].reshape(3, 3, patch_width, patch_width)
    weight_b = gathered[1].reshape(3, 3, patch_width, patch_width)
    film_row = lax.dynamic_index_in_dim(film, lead_ids[0], 0, keepdims=False)
    mult_a = 1.0 + film_row[0]
    shift_a = film_row[1]
    mult_b = 1.0 + film_row[2]
    shift_b = film_row[3]
    weather_field = inputs[0]
    input_kernel_taps = adjacent_cells(
        weather_field, FIRST_DILATION // tile_row_count, FIRST_DILATION // tile_column_count
    )
    input_columns, matrix_a = lower(input_kernel_taps, weight_a, False)
    pre_a = jnp.dot(input_columns, matrix_a, preferred_element_type=jnp.float32) * mult_a + shift_a
    sig_a = jax.nn.sigmoid(pre_a)
    hidden_state = (
        weather_field.reshape(-1, patch_width).astype(jnp.float32) + pre_a * sig_a
    ).astype(jnp.bfloat16)
    taps_hidden = adjacent_cells(
        hidden_state.reshape(tile_row_count, tile_column_count, patch_width),
        SECOND_DILATION // tile_row_count,
        SECOND_DILATION // tile_column_count,
    )
    hidden_columns, matrix_b = lower(taps_hidden, weight_b, False)
    pre_b = jnp.dot(hidden_columns, matrix_b, preferred_element_type=jnp.float32) * mult_b + shift_b
    sig_b = jax.nn.sigmoid(pre_b)
    outputs = (hidden_state.astype(jnp.float32) + pre_b * sig_b).astype(jnp.bfloat16)
    upstream = cotangent[0].reshape(-1, patch_width).astype(jnp.float32)
    second_gradient = (upstream * mult_b * sig_b * (1.0 + pre_b * (1.0 - sig_b))).astype(
        jnp.bfloat16
    )
    taps_grad = adjacent_cells(
        second_gradient.reshape(tile_row_count, tile_column_count, patch_width),
        SECOND_DILATION // tile_row_count,
        SECOND_DILATION // tile_column_count,
    )
    column_gradient, matrix_t = lower(taps_grad, weight_b, True)
    back = upstream + jnp.dot(column_gradient, matrix_t, preferred_element_type=jnp.float32)
    grad_a = (back * mult_a * sig_a * (1.0 + pre_a * (1.0 - sig_a))).astype(jnp.bfloat16)
    scale = 1.0 / math.sqrt(lax.axis_size(AXES) * tile_row_count * tile_column_count)
    products = (
        lax.dot_general(
            input_columns, grad_a, (((0,), (0,)), ((), ())), preferred_element_type=jnp.float32
        )
        * scale
    )
    term = jnp.zeros((3, 3, patch_width, patch_width), jnp.float32)
    for number, (row_off, col_off, piece) in enumerate(input_kernel_taps):
        term = term.at[row_off + 1, col_off + 1].set(
            products[number * patch_width : (number + 1) * patch_width]
        )
    flat_term = term.reshape(lax.axis_size(("lead", "gy")), lax.axis_size("gx"), -1)
    partial_sum = lax.psum_scatter(flat_term, "gx", scatter_dimension=1, tiled=True)
    total = lax.psum_scatter(partial_sum, ("lead", "gy"), scatter_dimension=0, tiled=True)
    return (outputs.reshape(inputs.shape), total.reshape(-1))


def fits(mesh, rows, columns):
    size = mesh.shape
    return (
        tuple(mesh.axis_names) == AXES
        and (size["lead"], size["gy"], size["gx"]) == (2, 4, 4)
        and FIRST_DILATION == rows
        and SECOND_DILATION == 2 * rows
        and FIRST_DILATION // columns >= size["gx"]
    )


def pairs(move):
    number = lambda x, y, c, z: x * 16 + (2 * y + c) * 4 + z
    return [
        (number(x, y, c, z), number(*move(x, y, c, z)))
        for x in range(2)
        for y in range(2)
        for c in range(2)
        for z in range(4)
    ]


def moved(value, dx=0, dy=0, dc=0, dz=0):
    return lax.ppermute(
        value, AXES, pairs(lambda x, y, c, z: (x ^ dx, y ^ dy, c ^ dc, z ^ dz))
    )


FIRST_ROUND = ((1, 2), (0, 2), (1, 0))
SECOND_ROUND = ((1, 1), (0, 1), (1, 0))


def place():
    x, gy, z = (lax.axis_index(axis) for axis in AXES)
    return x, gy // 2, gy % 2, z


def used_rows(width, shard_rows):
    found = []
    for block in range(3):
        start = (3 * block + 1) * width
        row = start
        while row < start + width:
            shard = row // shard_rows
            stop = min((shard + 1) * shard_rows, start + width)
            place = (shard // 16, shard // 8 % 2, shard // 4 % 2, shard % 4)
            found.append((*place, row - shard * shard_rows, stop - row, block * width + row - start))
            row = stop
    return found


def chosen(table, here, otherwise):
    value = otherwise
    for key, entry in table.items():
        if entry != otherwise:
            match = here[0] == key[0]
            for mine, wanted in zip(here[1:], key[1:]):
                match = match & (mine == wanted)
            value = jnp.where(match, entry, value)
    return value


class Layout:
    def __init__(self, width, shard_rows):
        self.pieces = {(x, part): [] for x in range(2) for part in range(2)}
        self.base, self.first, self.stop = {}, {}, {}
        held = dict.fromkeys(self.pieces, 0)
        for cx, cy, cc, cz, first, count, row in used_rows(width, shard_rows):
            group, key = (cx, cz % 2), (cx, cy, cz, cc)
            assert key not in self.base
            self.pieces[group].append((held[group], count, row))
            self.base[key] = held[group] - first
            self.first[key], self.stop[key] = first, first + count
            held[group] += count
        self.rows = max(held.values())
        self.low = {key[:3]: stop for key, stop in self.stop.items() if key[3] == 1}
        for key, first in self.first.items():
            assert key[3] == 1 or self.low.get(key[:3], 0) <= first


def copy_kernel(layout, value_ref, out_ref):
    out_ref[...] = value_ref[...]


def piece_kernel(layout, own_ref, near_ref, out_ref):
    x, y, c, z = place()
    lane = out_ref.shape[2]
    own, near = own_ref[...], near_ref[...]
    own = jnp.where(c == 0, own[:, :, :lane], own[:, :, lane:])
    near = jnp.where(c == 0, near[:, :, :lane], near[:, :, lane:])
    row = lax.broadcasted_iota(jnp.int32, out_ref.shape, 1)
    own_rows = (row < chosen(layout.low, (x, y, z), 0)) == (c == 1)
    out_ref[...] = jnp.where(own_rows, own, near)


def group_kernel(layout, own_ref, far0_ref, far1_ref, far2_ref, out_ref, total):
    x, y, c, z = place()
    rows = own_ref.shape[1]
    total[...] = jnp.zeros_like(total)
    row = lax.broadcasted_iota(jnp.int32, own_ref.shape[1:], 0)
    for (dy, dz), ref in zip(((0, 0), *FIRST_ROUND), (own_ref, far0_ref, far1_ref, far2_ref)):
        for core in range(2):
            here = (x, y ^ dy, z ^ dz, core)
            first, stop = chosen(layout.first, here, 0), chosen(layout.stop, here, 0)
            base = pl.multiple_of(rows + chosen(layout.base, here, -rows), 8)
            used = (row >= first) & (row < stop)
            for k in range(2):
                value = jnp.where(used, ref[k].astype(jnp.float32), 0.0)
                total[k, pl.ds(base, rows), :] += value
    out_ref[...] = total[:, rows : rows + out_ref.shape[1], :].astype(out_ref.dtype)


def slot(dx, dz):
    found = 0
    for number, (to_x, to_z) in enumerate(SECOND_ROUND):
        found = jnp.where((dx == to_x) & (dz == to_z), number + 1, found)
    return found


def order_kernel(layout, own_ref, far0_ref, far1_ref, far2_ref, a_ref, b_ref, held, total):
    x, y, c, z = place()
    for number, ref in enumerate((own_ref, far0_ref, far1_ref, far2_ref)):
        held[number] = ref[...].astype(jnp.float32)
    for (cx, part), pieces in layout.pieces.items():
        number = slot(cx ^ x, part ^ (z % 2))
        for start, count, row in pieces:
            total[:, row : row + count, :] = held[number, :, start : start + count, :]
    a_ref[...] = total[0].astype(a_ref.dtype)
    b_ref[...] = total[1].astype(b_ref.dtype)


def matrix(own_ref, near_ref):
    c = place()[2]
    own, near = own_ref[...], near_ref[...]
    return jnp.concatenate([jnp.where(c == 0, own, near), jnp.where(c == 0, near, own)], axis=1)


def dot(a, b, dims=((1,), (0,))):
    return lax.dot_general(a, b, (dims, ((), ())), preferred_element_type=jnp.float32)


def first_kernel(
    layout, mine_ref, other_ref, near0_ref, near1_ref, own_w, near_w, film_ref,
    field_ref, slope_ref, hidden_ref,
):
    x, y, c, z = place()
    half, width = mine_ref.shape
    near0, near1 = near0_ref[...], near1_ref[...]
    mine, other = mine_ref[...], other_ref[0]
    lo, hi = jnp.where(y == 0, mine, other), jnp.where(y == 0, other, mine)
    near_lo, near_hi = jnp.where(y == 0, near0, near1), jnp.where(y == 0, near1, near0)
    field_ref[0] = jnp.zeros_like(lo)
    field_ref[1] = jnp.where(c == 0, lo, near_lo)
    field_ref[2] = jnp.where(c == 0, near_lo, lo)
    field_ref[3] = jnp.where(c == 0, hi, near_hi)
    field_ref[4] = jnp.where(c == 0, near_hi, hi)
    field_ref[5] = jnp.zeros_like(lo)
    above = jnp.concatenate([field_ref[c], field_ref[c + 2]], axis=0)
    mid = jnp.concatenate([lo, hi], axis=0)
    below = jnp.concatenate([field_ref[c + 2], field_ref[c + 4]], axis=0)
    weight = matrix(own_w, near_w)
    conv = dot(above, weight[:width]) + dot(mid, weight[width : 2 * width])
    conv = conv + dot(below, weight[2 * width :])
    pre = conv * (1.0 + film_ref[0:1, :]) + film_ref[1:2, :]
    sig = jax.nn.sigmoid(pre)
    lift = pre * sig
    hidden_ref[...] = (mid.astype(jnp.float32) + lift).astype(hidden_ref.dtype)
    slope_ref[...] = (1.0 + film_ref[0:1, :]) * (sig + lift * (1.0 - sig))


def second_kernel(
    layout, slope_ref, hidden_ref, mine_ct, other_ref, own_w, near_w, film_ref,
    out_keep, out_send, grad_keep, grad_send,
):
    x, y, c, z = place()
    half, width = mine_ct.shape
    f32, bf16 = jnp.float32, jnp.bfloat16
    lane = width // 2
    mult_b = 1.0 + film_ref[2:3, :]
    weight = matrix(own_w, near_w)
    up, centre, down = weight[:width], weight[width : 2 * width], weight[2 * width :]
    hidden = hidden_ref[...]
    across = jnp.concatenate([dot(hidden[half:], down), dot(hidden[:half], up)], axis=0)
    pre_b = (dot(hidden, centre) + across) * mult_b + film_ref[3:4, :]
    sig_b = jax.nn.sigmoid(pre_b)
    lift_b = pre_b * sig_b
    result = (hidden.astype(f32) + lift_b).astype(bf16)
    out_keep[...] = jnp.where(y == 0, result[:half], result[half:])
    out_send[...] = jnp.where(y == 0, result[half:], result[:half])
    mine, other = mine_ct[...], other_ref[1]
    lo, hi = jnp.where(y == 0, mine, other), jnp.where(y == 0, other, mine)
    upstream = jnp.concatenate([lo, hi], axis=0).astype(f32)
    grad_b = (upstream * (mult_b * (sig_b + lift_b * (1.0 - sig_b)))).astype(bf16)
    turned = ((1,), (1,))
    back = jnp.concatenate(
        [dot(grad_b[half:], up, turned), dot(grad_b[:half], down, turned)], axis=0
    )
    back = upstream + dot(grad_b, centre, turned) + back
    grad_a = (back * slope_ref[...]).astype(bf16)
    grad_keep[...] = jnp.where(c == 0, grad_a[:, :lane], grad_a[:, lane:])
    grad_send[...] = jnp.where(c == 0, grad_a[:, lane:], grad_a[:, :lane])


def term_kernel(
    layout, scale, field_ref, keep_ref, near_ref, own_ref, far0_ref, far1_ref, far2_ref, total, groups
):
    x, y, c, z = place()
    half, width = field_ref.shape[1:]
    keep, near = keep_ref[...], near_ref[...]
    even, odd = jnp.where(c == 0, keep, near), jnp.where(c == 0, near, keep)
    grad = jnp.concatenate([even[:half], odd[:half], even[half:], odd[half:]], axis=0)
    field = jnp.concatenate([field_ref[tile] for tile in range(1, 5)], axis=0)
    none = jnp.zeros_like(grad[:half])
    below = jnp.concatenate([grad[half:], none], axis=0)
    above = jnp.concatenate([none, grad[: 3 * half]], axis=0)
    sums = dot(field, jnp.concatenate([below, grad, above], axis=1), ((0,), (0,))) * scale
    lane = width // 2
    for number in range(3):
        total[number * width : (number + 1) * width, :] = sums[:, number * lane : (number + 1) * lane]
    for number, pieces in enumerate(layout.pieces.values()):
        for start, count, row in pieces:
            groups[number, start : start + count, :] = total[row : row + count, :]
    for (dx, dz), ref in zip(((0, 0), *SECOND_ROUND), (own_ref, far0_ref, far1_ref, far2_ref)):
        number = 2 * (x ^ dx) + (z ^ dz) % 2
        ref[...] = groups[number].astype(ref.dtype)


def chip_kernel(layout, own_ref, far0_ref, far1_ref, far2_ref, out0, out1, out2, out3, total):
    x, y, c, z = place()
    f32 = jnp.float32
    rows, lane = own_ref.shape
    piece_rows = out0.shape[0]
    value = own_ref[...]
    for ref in (far0_ref, far1_ref, far2_ref):
        value = value + ref[...].astype(f32)
    edge = jnp.zeros((piece_rows, lane), f32)
    total[0:piece_rows, :] = edge
    total[piece_rows : piece_rows + rows, :] = value
    total[piece_rows + rows :, :] = edge
    row = lax.broadcasted_iota(jnp.int32, out0.shape, 0)
    for (dy, dz), ref in zip(((0, 0), *FIRST_ROUND), (out0, out1, out2, out3)):
        piece = edge
        for core in range(2):
            here = (x, y ^ dy, z ^ dz, core)
            base = piece_rows + chosen(layout.base, here, -piece_rows)
            used = (row >= chosen(layout.first, here, 0)) & (row < chosen(layout.stop, here, 0))
            piece = jnp.where(used, total[pl.ds(pl.multiple_of(base, 8), piece_rows), :], piece)
        ref[...] = piece.astype(ref.dtype)


def last_kernel(layout, own_ref, other_ref, out_ref):
    x, y, c, z = place()
    rows = own_ref.shape[0]
    row = lax.broadcasted_iota(jnp.int32, own_ref.shape, 0)
    held = jnp.logical_xor(row < chosen(layout.low, (x, y, z), 0), c == 0)
    own = jnp.where(held, own_ref[...], 0.0)
    other = jnp.where(held, other_ref[...], 0.0)
    out_ref[pl.ds(0, rows, stride=2), :] = jnp.where(c == 0, own, other)
    out_ref[pl.ds(1, rows, stride=2), :] = jnp.where(c == 0, other, own)


def row_shards(inputs, lead_ids, film, flat_weights, cotangent):
    rows, columns, width = inputs.shape[1:]
    half = rows // 2 * columns
    lane = width // 2
    shard_rows = flat_weights.shape[1] // width
    x, y, c, z = place()
    layout = Layout(width, shard_rows)
    bf16, f32 = jnp.bfloat16, jnp.float32
    shape = jax.ShapeDtypeStruct

    def call(name, body, out_shape, scratch, *operands, cost=0):
        vmem = pl.BlockSpec(memory_space=pltpu.VMEM)
        several = isinstance(out_shape, tuple)
        return pl.pallas_call(
            lambda *refs: body(layout, *refs),
            out_shape=out_shape,
            in_specs=[vmem] * len(operands),
            out_specs=(vmem,) * len(out_shape) if several else vmem,
            scratch_shapes=scratch,
            compiler_params=pltpu.CompilerParams(vmem_limit_bytes=16 * 1024 * 1024),
            cost_estimate=pl.CostEstimate(flops=cost * 10**9, bytes_accessed=0, transcendentals=0) if cost else None,
            name=name,
        )(*operands)

    shard = flat_weights.reshape(2, shard_rows, width)
    near = moved(flat_weights, dc=1).reshape(shard.shape)
    piece = call("piece", piece_kernel, shape((2, shard_rows, lane), bf16), [], shard, near)

    halves_x, halves_ct = (array.reshape(2, half, width) for array in (inputs, cotangent))
    pick = lambda halves, number: lax.dynamic_index_in_dim(halves, number, 0, keepdims=False)
    piece, halves_x, halves_ct = lax.optimization_barrier((piece, halves_x, halves_ct))
    give = jnp.stack([pick(halves_x, 1 - y), pick(halves_ct, 1 - y)])
    give = call("give", copy_kernel, shape(give.shape, bf16), [], give, cost=3)
    other = moved(give, dy=1)
    line = [piece, *(moved(piece, dy=dy, dz=dz) for dy, dz in FIRST_ROUND)]
    *line, halves_x, halves_ct, film = lax.optimization_barrier(
        (*line, halves_x, halves_ct, film)
    )
    mine_x, mine_ct = pick(halves_x, y), pick(halves_ct, y)
    film_row = lax.dynamic_index_in_dim(film, lead_ids[0], 0, keepdims=False)
    near_x0 = moved(mine_x, dc=1)
    group = call(
        "group",
        group_kernel,
        shape((2, layout.rows, lane), bf16),
        [pltpu.VMEM((2, layout.rows + 2 * shard_rows, lane), f32)],
        *line,
        cost=6,
    )
    near_x1 = moved(other[0], dc=1)
    groups = [group, *(moved(group, dx=dx, dz=dz) for dx, dz in SECOND_ROUND)]
    *groups, near_x0, near_x1, mine_x, mine_ct, film_row = lax.optimization_barrier(
        (*groups, near_x0, near_x1, mine_x, mine_ct, film_row)
    )
    own_a, own_b = call(
        "order",
        order_kernel,
        (shape((3 * width, lane), bf16),) * 2,
        [pltpu.VMEM((4, 2, layout.rows, lane), f32), pltpu.VMEM((2, 3 * width, lane), f32)],
        *groups,
    )
    near_a, near_b = moved(own_a, dc=1), moved(own_b, dc=1)

    field, slope_a, hidden = call(
        "block_one",
        first_kernel,
        (shape((6, half, width), bf16), shape((2 * half, width), f32), shape((2 * half, width), bf16)),
        [],
        *(mine_x, other, near_x0, near_x1, own_a, near_a, film_row),
    )
    out_keep, out_send, grad_keep, grad_send = call(
        "block_two",
        second_kernel,
        (shape((half, width), bf16),) * 2 + (shape((2 * half, lane), bf16),) * 2,
        [],
        *(slope_a, hidden, mine_ct, other, own_b, near_b, film_row),
    )

    scale = 1.0 / math.sqrt(lax.axis_size(AXES) * rows * columns)
    terms = call(
        "terms",
        lambda layout, *refs: term_kernel(layout, scale, *refs),
        (shape((layout.rows, lane), f32),) + (shape((layout.rows, lane), bf16),) * 3,
        [pltpu.VMEM((3 * width, lane), f32), pltpu.VMEM((4, layout.rows, lane), f32)],
        *(field, grad_keep, moved(grad_send, dc=1)),
    )
    other_out = moved(out_send, dy=1)
    terms = [terms[0], *(moved(term, dx=dx, dz=dz) for term, (dx, dz) in zip(terms[1:], SECOND_ROUND))]
    chip = call(
        "chips",
        chip_kernel,
        (shape((shard_rows, lane), f32),) + (shape((shard_rows, lane), bf16),) * 3,
        [pltpu.VMEM((layout.rows + 2 * shard_rows, lane), f32)],
        *terms,
    )
    lane_sum = chip[0]
    for term, (dy, dz) in zip(chip[1:], FIRST_ROUND):
        lane_sum = lane_sum + moved(term, dy=dy, dz=dz).astype(f32)

    first = jnp.where(y == 0, out_keep, other_out)
    second = jnp.where(y == 0, other_out, out_keep)
    outputs = jnp.stack([first, second]).reshape(inputs.shape)

    total = call(
        "total",
        last_kernel,
        shape((2 * shard_rows, lane), f32),
        [],
        *(lane_sum, moved(lane_sum, dc=1)),
    )
    return (outputs, total.reshape(-1))


def solution(mesh):
    def whole(inputs, lead_ids, film, flat_weights, cotangent):
        size = mesh.shape
        rows, columns = inputs.shape[1] // size["gy"], inputs.shape[2] // size["gx"]
        plan = row_shards if fits(mesh, rows, columns) else general_shards
        return jax.shard_map(
            plan,
            mesh=mesh,
            in_specs=(
                P("lead", "gy", "gx", None),
                P("lead"),
                P(),
                P(None, AXES),
                P("lead", "gy", "gx", None),
            ),
            out_specs=(P("lead", "gy", "gx", None), P(AXES)),
            check_vma=False,
        )(inputs, lead_ids, film, flat_weights, cotangent)

    return whole
```

```python
import math

import jax
import jax.numpy as jnp
from jax import lax
from jax.experimental import pallas as pl
from jax.experimental.pallas import tpu as pltpu
from jax.sharding import PartitionSpec as P

FIRST_DILATION = 64
SECOND_DILATION = 128
AXES = ("lead", "gy", "gx")


def passed_along(value, axis, steps):
    count = lax.axis_size(axis)
    leading, last = (max(0, -steps), min(count, count - steps))
    return lax.ppermute(value, axis, [(source, source + steps) for source in range(leading, last)])


def shortened(array):
    return jax.tree.map(lambda a: a.astype(jnp.bfloat16) if a.dtype == jnp.float32 else a, array)


def adjacent_cells(weather_field, row_step, col_step):
    row_list = [-1, 0, 1]
    col_list = [-1, 0, 1] if col_step < lax.axis_size("gx") else [0]
    taps = []
    stacked = jnp.stack(
        [
            (
                weather_field
                if row_off == 0
                else passed_along(weather_field, "gy", -row_off * row_step)
            )
            for row_off in row_list
        ]
    )
    columns = [
        (
            stacked
            if col_off == 0
            else passed_along(shortened(stacked), "gx", -col_off * col_step).astype(stacked.dtype)
        )
        for col_off in col_list
    ]
    for col_off in col_list:
        for row_off in row_list:
            taps.append(
                (row_off, col_off, columns[col_list.index(col_off)][row_list.index(row_off)])
            )
    return taps


def lower(taps, weight_four, flipped):
    patch_width = weight_four.shape[-1]
    cols = jnp.concatenate(
        [piece.reshape(-1, patch_width) for row_off, col_off, piece in taps], axis=1
    )
    blocks = []
    for row_off, col_off, piece in taps:
        if flipped:
            blocks.append(weight_four[1 - row_off, 1 - col_off].T)
        else:
            blocks.append(weight_four[row_off + 1, col_off + 1])
    return (cols, jnp.concatenate(blocks, axis=0))


def general_shards(inputs, lead_ids, film, flat_weights, cotangent):
    tile_row_count, tile_column_count, patch_width = (
        inputs.shape[1],
        inputs.shape[2],
        inputs.shape[3],
    )
    gathered = lax.all_gather(flat_weights, AXES, axis=1, tiled=True)
    weight_a = gathered[0].reshape(3, 3, patch_width, patch_width)
    weight_b = gathered[1].reshape(3, 3, patch_width, patch_width)
    film_row = lax.dynamic_index_in_dim(film, lead_ids[0], 0, keepdims=False)
    mult_a = 1.0 + film_row[0]
    shift_a = film_row[1]
    mult_b = 1.0 + film_row[2]
    shift_b = film_row[3]
    weather_field = inputs[0]
    input_kernel_taps = adjacent_cells(
        weather_field, FIRST_DILATION // tile_row_count, FIRST_DILATION // tile_column_count
    )
    input_columns, matrix_a = lower(input_kernel_taps, weight_a, False)
    pre_a = jnp.dot(input_columns, matrix_a, preferred_element_type=jnp.float32) * mult_a + shift_a
    sig_a = jax.nn.sigmoid(pre_a)
    hidden_state = (
        weather_field.reshape(-1, patch_width).astype(jnp.float32) + pre_a * sig_a
    ).astype(jnp.bfloat16)
    taps_hidden = adjacent_cells(
        hidden_state.reshape(tile_row_count, tile_column_count, patch_width),
        SECOND_DILATION // tile_row_count,
        SECOND_DILATION // tile_column_count,
    )
    hidden_columns, matrix_b = lower(taps_hidden, weight_b, False)
    pre_b = jnp.dot(hidden_columns, matrix_b, preferred_element_type=jnp.float32) * mult_b + shift_b
    sig_b = jax.nn.sigmoid(pre_b)
    outputs = (hidden_state.astype(jnp.float32) + pre_b * sig_b).astype(jnp.bfloat16)
    upstream = cotangent[0].reshape(-1, patch_width).astype(jnp.float32)
    second_gradient = (upstream * mult_b * sig_b * (1.0 + pre_b * (1.0 - sig_b))).astype(
        jnp.bfloat16
    )
    taps_grad = adjacent_cells(
        second_gradient.reshape(tile_row_count, tile_column_count, patch_width),
        SECOND_DILATION // tile_row_count,
        SECOND_DILATION // tile_column_count,
    )
    column_gradient, matrix_t = lower(taps_grad, weight_b, True)
    back = upstream + jnp.dot(column_gradient, matrix_t, preferred_element_type=jnp.float32)
    grad_a = (back * mult_a * sig_a * (1.0 + pre_a * (1.0 - sig_a))).astype(jnp.bfloat16)
    scale = 1.0 / math.sqrt(lax.axis_size(AXES) * tile_row_count * tile_column_count)
    products = (
        lax.dot_general(
            input_columns, grad_a, (((0,), (0,)), ((), ())), preferred_element_type=jnp.float32
        )
        * scale
    )
    term = jnp.zeros((3, 3, patch_width, patch_width), jnp.float32)
    for number, (row_off, col_off, piece) in enumerate(input_kernel_taps):
        term = term.at[row_off + 1, col_off + 1].set(
            products[number * patch_width : (number + 1) * patch_width]
        )
    flat_term = term.reshape(lax.axis_size(("lead", "gy")), lax.axis_size("gx"), -1)
    partial_sum = lax.psum_scatter(flat_term, "gx", scatter_dimension=1, tiled=True)
    total = lax.psum_scatter(partial_sum, ("lead", "gy"), scatter_dimension=0, tiled=True)
    return (outputs.reshape(inputs.shape), total.reshape(-1))


def fits(mesh, rows, columns):
    size = mesh.shape
    return (
        tuple(mesh.axis_names) == AXES
        and (size["lead"], size["gy"], size["gx"]) == (2, 4, 4)
        and FIRST_DILATION == rows
        and SECOND_DILATION == 2 * rows
        and FIRST_DILATION // columns >= size["gx"]
    )


def pairs(move):
    number = lambda x, y, c, z: x * 16 + (2 * y + c) * 4 + z
    return [
        (number(x, y, c, z), number(*move(x, y, c, z)))
        for x in range(2)
        for y in range(2)
        for c in range(2)
        for z in range(4)
    ]


def moved(value, dx=0, dy=0, dc=0, dz=0):
    return lax.ppermute(
        value, AXES, pairs(lambda x, y, c, z: (x ^ dx, y ^ dy, c ^ dc, z ^ dz))
    )


FIRST_ROUND = ((1, 2), (0, 2), (1, 0))
SECOND_ROUND = ((1, 1), (0, 1), (1, 0))


def place():
    x, gy, z = (lax.axis_index(axis) for axis in AXES)
    return x, gy // 2, gy % 2, z


def used_rows(width, shard_rows):
    found = []
    for block in range(3):
        start = (3 * block + 1) * width
        row = start
        while row < start + width:
            shard = row // shard_rows
            stop = min((shard + 1) * shard_rows, start + width)
            place = (shard // 16, shard // 8 % 2, shard // 4 % 2, shard % 4)
            found.append((*place, row - shard * shard_rows, stop - row, block * width + row - start))
            row = stop
    return found


def chosen(table, here, otherwise):
    value = otherwise
    for key, entry in table.items():
        if entry != otherwise:
            match = here[0] == key[0]
            for mine, wanted in zip(here[1:], key[1:]):
                match = match & (mine == wanted)
            value = jnp.where(match, entry, value)
    return value


class Layout:
    def __init__(self, width, shard_rows):
        self.pieces = {(x, part): [] for x in range(2) for part in range(2)}
        self.base, self.first, self.stop = {}, {}, {}
        held = dict.fromkeys(self.pieces, 0)
        for cx, cy, cc, cz, first, count, row in used_rows(width, shard_rows):
            group, key = (cx, cz % 2), (cx, cy, cz, cc)
            assert key not in self.base
            self.pieces[group].append((held[group], count, row))
            self.base[key] = held[group] - first
            self.first[key], self.stop[key] = first, first + count
            held[group] += count
        self.rows = max(held.values())
        self.low = {key[:3]: stop for key, stop in self.stop.items() if key[3] == 1}
        for key, first in self.first.items():
            assert key[3] == 1 or self.low.get(key[:3], 0) <= first


def copy_kernel(layout, value_ref, out_ref):
    out_ref[...] = value_ref[...]


def piece_kernel(layout, own_ref, near_ref, out_ref):
    x, y, c, z = place()
    lane = out_ref.shape[2]
    own, near = own_ref[...], near_ref[...]
    own = jnp.where(c == 0, own[:, :, :lane], own[:, :, lane:])
    near = jnp.where(c == 0, near[:, :, :lane], near[:, :, lane:])
    row = lax.broadcasted_iota(jnp.int32, out_ref.shape, 1)
    own_rows = (row < chosen(layout.low, (x, y, z), 0)) == (c == 1)
    out_ref[...] = jnp.where(own_rows, own, near)


def group_kernel(layout, own_ref, far0_ref, far1_ref, far2_ref, out_ref, total):
    x, y, c, z = place()
    rows = own_ref.shape[1]
    total[...] = jnp.zeros_like(total)
    row = lax.broadcasted_iota(jnp.int32, own_ref.shape[1:], 0)
    for (dy, dz), ref in zip(((0, 0), *FIRST_ROUND), (own_ref, far0_ref, far1_ref, far2_ref)):
        for core in range(2):
            here = (x, y ^ dy, z ^ dz, core)
            first, stop = chosen(layout.first, here, 0), chosen(layout.stop, here, 0)
            base = pl.multiple_of(rows + chosen(layout.base, here, -rows), 8)
            used = (row >= first) & (row < stop)
            for k in range(2):
                value = jnp.where(used, ref[k].astype(jnp.float32), 0.0)
                total[k, pl.ds(base, rows), :] += value
    out_ref[...] = total[:, rows : rows + out_ref.shape[1], :].astype(out_ref.dtype)


def slot(dx, dz):
    found = 0
    for number, (to_x, to_z) in enumerate(SECOND_ROUND):
        found = jnp.where((dx == to_x) & (dz == to_z), number + 1, found)
    return found


def order_kernel(layout, own_ref, far0_ref, far1_ref, far2_ref, a_ref, b_ref, held, total):
    x, y, c, z = place()
    for number, ref in enumerate((own_ref, far0_ref, far1_ref, far2_ref)):
        held[number] = ref[...].astype(jnp.float32)
    for (cx, part), pieces in layout.pieces.items():
        number = slot(cx ^ x, part ^ (z % 2))
        for start, count, row in pieces:
            total[:, row : row + count, :] = held[number, :, start : start + count, :]
    a_ref[...] = total[0].astype(a_ref.dtype)
    b_ref[...] = total[1].astype(b_ref.dtype)


def matrix(own_ref, near_ref):
    c = place()[2]
    own, near = own_ref[...], near_ref[...]
    return jnp.concatenate([jnp.where(c == 0, own, near), jnp.where(c == 0, near, own)], axis=1)


def dot(a, b, dims=((1,), (0,))):
    return lax.dot_general(a, b, (dims, ((), ())), preferred_element_type=jnp.float32)


def first_kernel(
    layout, mine_ref, other_ref, near0_ref, near1_ref, own_w, near_w, film_ref,
    field_ref, slope_ref, hidden_ref,
):
    x, y, c, z = place()
    half, width = mine_ref.shape
    near0, near1 = near0_ref[...], near1_ref[...]
    mine, other = mine_ref[...], other_ref[0]
    lo, hi = jnp.where(y == 0, mine, other), jnp.where(y == 0, other, mine)
    near_lo, near_hi = jnp.where(y == 0, near0, near1), jnp.where(y == 0, near1, near0)
    field_ref[0] = jnp.zeros_like(lo)
    field_ref[1] = jnp.where(c == 0, lo, near_lo)
    field_ref[2] = jnp.where(c == 0, near_lo, lo)
    field_ref[3] = jnp.where(c == 0, hi, near_hi)
    field_ref[4] = jnp.where(c == 0, near_hi, hi)
    field_ref[5] = jnp.zeros_like(lo)
    above = jnp.concatenate([field_ref[c], field_ref[c + 2]], axis=0)
    mid = jnp.concatenate([lo, hi], axis=0)
    below = jnp.concatenate([field_ref[c + 2], field_ref[c + 4]], axis=0)
    weight = matrix(own_w, near_w)
    conv = dot(above, weight[:width]) + dot(mid, weight[width : 2 * width])
    conv = conv + dot(below, weight[2 * width :])
    pre = conv * (1.0 + film_ref[0:1, :]) + film_ref[1:2, :]
    sig = jax.nn.sigmoid(pre)
    lift = pre * sig
    hidden_ref[...] = (mid.astype(jnp.float32) + lift).astype(hidden_ref.dtype)
    slope_ref[...] = (1.0 + film_ref[0:1, :]) * (sig + lift * (1.0 - sig))


def second_kernel(
    layout, slope_ref, hidden_ref, mine_ct, other_ref, own_w, near_w, film_ref,
    out_keep, out_send, grad_keep, grad_send,
):
    x, y, c, z = place()
    half, width = mine_ct.shape
    f32, bf16 = jnp.float32, jnp.bfloat16
    lane = width // 2
    mult_b = 1.0 + film_ref[2:3, :]
    weight = matrix(own_w, near_w)
    up, centre, down = weight[:width], weight[width : 2 * width], weight[2 * width :]
    hidden = hidden_ref[...]
    across = jnp.concatenate([dot(hidden[half:], down), dot(hidden[:half], up)], axis=0)
    pre_b = (dot(hidden, centre) + across) * mult_b + film_ref[3:4, :]
    sig_b = jax.nn.sigmoid(pre_b)
    lift_b = pre_b * sig_b
    result = (hidden.astype(f32) + lift_b).astype(bf16)
    out_keep[...] = jnp.where(y == 0, result[:half], result[half:])
    out_send[...] = jnp.where(y == 0, result[half:], result[:half])
    mine, other = mine_ct[...], other_ref[1]
    lo, hi = jnp.where(y == 0, mine, other), jnp.where(y == 0, other, mine)
    upstream = jnp.concatenate([lo, hi], axis=0).astype(f32)
    grad_b = (upstream * (mult_b * (sig_b + lift_b * (1.0 - sig_b)))).astype(bf16)
    turned = ((1,), (1,))
    back = jnp.concatenate(
        [dot(grad_b[half:], up, turned), dot(grad_b[:half], down, turned)], axis=0
    )
    back = upstream + dot(grad_b, centre, turned) + back
    grad_a = (back * slope_ref[...]).astype(bf16)
    grad_keep[...] = jnp.where(c == 0, grad_a[:, :lane], grad_a[:, lane:])
    grad_send[...] = jnp.where(c == 0, grad_a[:, lane:], grad_a[:, :lane])


def term_kernel(
    layout, scale, field_ref, keep_ref, near_ref, own_ref, far0_ref, far1_ref, far2_ref, total, groups
):
    x, y, c, z = place()
    half, width = field_ref.shape[1:]
    keep, near = keep_ref[...], near_ref[...]
    even, odd = jnp.where(c == 0, keep, near), jnp.where(c == 0, near, keep)
    grad = jnp.concatenate([even[:half], odd[:half], even[half:], odd[half:]], axis=0)
    field = jnp.concatenate([field_ref[tile] for tile in range(1, 5)], axis=0)
    none = jnp.zeros_like(grad[:half])
    below = jnp.concatenate([grad[half:], none], axis=0)
    above = jnp.concatenate([none, grad[: 3 * half]], axis=0)
    sums = dot(field, jnp.concatenate([below, grad, above], axis=1), ((0,), (0,))) * scale
    lane = width // 2
    for number in range(3):
        total[number * width : (number + 1) * width, :] = sums[:, number * lane : (number + 1) * lane]
    for number, pieces in enumerate(layout.pieces.values()):
        for start, count, row in pieces:
            groups[number, start : start + count, :] = total[row : row + count, :]
    for (dx, dz), ref in zip(((0, 0), *SECOND_ROUND), (own_ref, far0_ref, far1_ref, far2_ref)):
        number = 2 * (x ^ dx) + (z ^ dz) % 2
        ref[...] = groups[number].astype(ref.dtype)


def chip_kernel(layout, own_ref, far0_ref, far1_ref, far2_ref, out0, out1, out2, out3, total):
    x, y, c, z = place()
    f32 = jnp.float32
    rows, lane = own_ref.shape
    piece_rows = out0.shape[0]
    value = own_ref[...]
    for ref in (far0_ref, far1_ref, far2_ref):
        value = value + ref[...].astype(f32)
    edge = jnp.zeros((piece_rows, lane), f32)
    total[0:piece_rows, :] = edge
    total[piece_rows : piece_rows + rows, :] = value
    total[piece_rows + rows :, :] = edge
    row = lax.broadcasted_iota(jnp.int32, out0.shape, 0)
    for (dy, dz), ref in zip(((0, 0), *FIRST_ROUND), (out0, out1, out2, out3)):
        piece = edge
        for core in range(2):
            here = (x, y ^ dy, z ^ dz, core)
            base = piece_rows + chosen(layout.base, here, -piece_rows)
            used = (row >= chosen(layout.first, here, 0)) & (row < chosen(layout.stop, here, 0))
            piece = jnp.where(used, total[pl.ds(pl.multiple_of(base, 8), piece_rows), :], piece)
        ref[...] = piece.astype(ref.dtype)


def last_kernel(layout, own_ref, other_ref, out_ref):
    x, y, c, z = place()
    rows = own_ref.shape[0]
    row = lax.broadcasted_iota(jnp.int32, own_ref.shape, 0)
    held = jnp.logical_xor(row < chosen(layout.low, (x, y, z), 0), c == 0)
    own = jnp.where(held, own_ref[...], 0.0)
    other = jnp.where(held, other_ref[...], 0.0)
    out_ref[pl.ds(0, rows, stride=2), :] = jnp.where(c == 0, own, other)
    out_ref[pl.ds(1, rows, stride=2), :] = jnp.where(c == 0, other, own)


def row_shards(inputs, lead_ids, film, flat_weights, cotangent):
    rows, columns, width = inputs.shape[1:]
    half = rows // 2 * columns
    lane = width // 2
    shard_rows = flat_weights.shape[1] // width
    x, y, c, z = place()
    layout = Layout(width, shard_rows)
    bf16, f32 = jnp.bfloat16, jnp.float32
    shape = jax.ShapeDtypeStruct

    def call(name, body, out_shape, scratch, *operands, cost=0):
        vmem = pl.BlockSpec(memory_space=pltpu.VMEM)
        several = isinstance(out_shape, tuple)
        return pl.pallas_call(
            lambda *refs: body(layout, *refs),
            out_shape=out_shape,
            in_specs=[vmem] * len(operands),
            out_specs=(vmem,) * len(out_shape) if several else vmem,
            scratch_shapes=scratch,
            compiler_params=pltpu.CompilerParams(vmem_limit_bytes=32 * 1024 * 1024),
            cost_estimate=pl.CostEstimate(flops=cost * 10**9, bytes_accessed=0, transcendentals=0) if cost else None,
            name=name,
        )(*operands)

    held = call("hold", copy_kernel, shape(flat_weights.shape, bf16), [], flat_weights)
    shard = held.reshape(2, shard_rows, width)
    near = moved(flat_weights, dc=1).reshape(shard.shape)
    piece = call("piece", piece_kernel, shape((2, shard_rows, lane), bf16), [], shard, near)

    halves_x, halves_ct = (array.reshape(2, half, width) for array in (inputs, cotangent))
    pick = lambda halves, number: lax.dynamic_index_in_dim(halves, number, 0, keepdims=False)
    piece, halves_x, halves_ct = lax.optimization_barrier((piece, halves_x, halves_ct))
    give = jnp.stack([pick(halves_x, 1 - y), pick(halves_ct, 1 - y)])
    give = call("give", copy_kernel, shape(give.shape, bf16), [], give, cost=3)
    other = moved(give, dy=1)
    line = [piece, *(moved(piece, dy=dy, dz=dz) for dy, dz in FIRST_ROUND)]
    *line, halves_x, halves_ct, film = lax.optimization_barrier(
        (*line, halves_x, halves_ct, film)
    )
    mine_x, mine_ct = pick(halves_x, y), pick(halves_ct, y)
    film_row = lax.dynamic_index_in_dim(film, lead_ids[0], 0, keepdims=False)
    near_x0 = moved(mine_x, dc=1)
    group = call(
        "group",
        group_kernel,
        shape((2, layout.rows, lane), bf16),
        [pltpu.VMEM((2, layout.rows + 2 * shard_rows, lane), f32)],
        *line,
        cost=6,
    )
    near_x1 = moved(other[0], dc=1)
    groups = [group, *(moved(group, dx=dx, dz=dz) for dx, dz in SECOND_ROUND)]
    *groups, near_x0, near_x1, mine_x, mine_ct, film_row = lax.optimization_barrier(
        (*groups, near_x0, near_x1, mine_x, mine_ct, film_row)
    )
    own_a, own_b = call(
        "order",
        order_kernel,
        (shape((3 * width, lane), bf16),) * 2,
        [pltpu.VMEM((4, 2, layout.rows, lane), f32), pltpu.VMEM((2, 3 * width, lane), f32)],
        *groups,
    )
    near_a, near_b = moved(own_a, dc=1), moved(own_b, dc=1)

    field, slope_a, hidden = call(
        "block_one",
        first_kernel,
        (shape((6, half, width), bf16), shape((2 * half, width), f32), shape((2 * half, width), bf16)),
        [],
        *(mine_x, other, near_x0, near_x1, own_a, near_a, film_row),
    )
    out_keep, out_send, grad_keep, grad_send = call(
        "block_two",
        second_kernel,
        (shape((half, width), bf16),) * 2 + (shape((2 * half, lane), bf16),) * 2,
        [],
        *(slope_a, hidden, mine_ct, other, own_b, near_b, film_row),
    )

    scale = 1.0 / math.sqrt(lax.axis_size(AXES) * rows * columns)
    terms = call(
        "terms",
        lambda layout, *refs: term_kernel(layout, scale, *refs),
        (shape((layout.rows, lane), f32),) + (shape((layout.rows, lane), bf16),) * 3,
        [pltpu.VMEM((3 * width, lane), f32), pltpu.VMEM((4, layout.rows, lane), f32)],
        *(field, grad_keep, moved(grad_send, dc=1)),
    )
    other_out = moved(out_send, dy=1)
    terms = [terms[0], *(moved(term, dx=dx, dz=dz) for term, (dx, dz) in zip(terms[1:], SECOND_ROUND))]
    chip = call(
        "chips",
        chip_kernel,
        (shape((shard_rows, lane), f32),) + (shape((shard_rows, lane), bf16),) * 3,
        [pltpu.VMEM((layout.rows + 2 * shard_rows, lane), f32)],
        *terms,
    )
    lane_sum = chip[0]
    for term, (dy, dz) in zip(chip[1:], FIRST_ROUND):
        lane_sum = lane_sum + moved(term, dy=dy, dz=dz).astype(f32)

    first = jnp.where(y == 0, out_keep, other_out)
    second = jnp.where(y == 0, other_out, out_keep)
    outputs = jnp.stack([first, second]).reshape(inputs.shape)

    total = call(
        "total",
        last_kernel,
        shape((2 * shard_rows, lane), f32),
        [],
        *(lane_sum, moved(lane_sum, dc=1)),
    )
    return (outputs, total.reshape(-1))


def solution(mesh):
    def whole(inputs, lead_ids, film, flat_weights, cotangent):
        size = mesh.shape
        rows, columns = inputs.shape[1] // size["gy"], inputs.shape[2] // size["gx"]
        plan = row_shards if fits(mesh, rows, columns) else general_shards
        return jax.shard_map(
            plan,
            mesh=mesh,
            in_specs=(
                P("lead", "gy", "gx", None),
                P("lead"),
                P(),
                P(None, AXES),
                P("lead", "gy", "gx", None),
            ),
            out_specs=(P("lead", "gy", "gx", None), P(AXES)),
            check_vma=False,
        )(inputs, lead_ids, film, flat_weights, cotangent)

    return whole
```
